32 devices in a mesh: feed: 8 (over z, core), chan: 4 (over y, x).
Axes of the slice: x: 2, y: 2, z: 4, core: 2. Of those that a mesh axis runs over, the one named last changes fastest.
Arguments:
- raw_samples: bfloat16 [256, 90112], P(('feed', 'chan')), may hold values from -6 to 6
- stack_code: int32 [256, 256], P('feed'), may hold values from -382 to 381, as said below
- stack_owner: int32 [382], replicated, may hold values from 0 to 7, as said below
Outputs:
- visibilities: float32 [760, 2, 2048], P('feed', None, 'chan')
The draws below stay inside these ranges and needn't reach their ends.
Inputs may be any that keep to these rules, and one draw needn't show every extreme that they name: `stack_code`: entry [i, j] names the stack of the baseline from input i to input j: s when it has stack s's orientation, -1 - s when reversed. For i != j entry [j, i] is -1 minus entry [i, j]; the diagonal holds 0; every stack is named. `stack_owner`: no owner has more than 95 stacks, and one owner has exactly 95.
All inputs are finite; a program needn't handle non-finite values.
Results may differ from the reference program's by a relative error of at most 0.0083.
Values may be sent and summed in bfloat16 or wider, within the bound.
No kernel may reach another device: no remote copies, remote signals or barrier semaphores. Data moves between devices by JAX's collectives and lax.ppermute only.
A program may use at most 128 MiB of HBM per device.

```python
import math
import jax
import jax.numpy as jnp
from jax import lax

NS = 128
INPUTS = 256
SPECTRA = 4
TAPS = 8
FA = 64
FB = 128
FRAME = 8192
CHANS = 2048
SAMPLES = 90112
STACKS = 382
OWNERS = 8
CAP = 95


def draw_stack_code(key, part):
    position = jax.random.permutation(jax.random.fold_in(key, 11), INPUTS).astype(jnp.int32)
    cylinder = position // NS
    along_ns = position % NS
    offset_east = cylinder[None, :] - cylinder[:, None]
    offset_north = along_ns[None, :] - along_ns[:, None]
    forward = (offset_east > 0) | (offset_east == 0) & (offset_north > 0)
    canon_east = jnp.where(forward, offset_east, -offset_east)
    canon_north = jnp.where(forward, offset_north, -offset_north)
    stack_id = jnp.where(canon_east == 0, canon_north - 1, NS - 1 + (canon_east - 1) * (2 * NS - 1) + canon_north + NS - 1)
    return jnp.where(forward, stack_id, -1 - stack_id).astype(jnp.int32)


def draw_stack_owner(key, part):
    shuffled = jax.random.permutation(jax.random.fold_in(key, 21), STACKS)
    busiest = jax.random.randint(jax.random.fold_in(key, 22), (), 0, OWNERS)
    remain = STACKS - CAP
    spacing = remain // (OWNERS - 1)
    jitter = jax.random.randint(jax.random.fold_in(key, 23), (OWNERS - 2,), -(spacing // 4), spacing // 4 + 1)
    bounds = jnp.arange(1, OWNERS - 1) * remain // (OWNERS - 1) + jitter
    ranked = jnp.arange(STACKS) - CAP
    group_id = jnp.sum((ranked[:, None] >= bounds[None, :]).astype(jnp.int32), axis=1)
    others = jnp.where(group_id >= busiest, group_id + 1, group_id)
    assigned = jnp.where(ranked < 0, busiest, others).astype(jnp.int32)
    return jnp.zeros((STACKS,), jnp.int32).at[shuffled].set(assigned)


def block_levels(stream_key, dims, cuts, least, top_value):
    def one(dim, blocks):
        draws = jax.random.uniform(jax.random.fold_in(jax.random.fold_in(stream_key, 6), dim), (blocks,), jnp.float32, least / len(cuts), top_value / len(cuts))
        return jnp.repeat(jnp.exp(draws), dims[dim] // blocks).reshape((-1,) + (1,) * (len(dims) - dim - 1))

    loudness = one(*cuts[0])
    for cut in cuts[1:]:
        loudness = loudness * one(*cut)
    return loudness


def gaussian(key, dims, width, bound, cuts=(), kind=jnp.bfloat16):
    level = block_levels(key, dims, cuts, -0.22, 0.18) if cuts else 1.0
    result = jax.random.normal(key, dims, jnp.float32) * width * level
    return jnp.minimum(jnp.maximum(result, -bound), bound).astype(kind)


def setup_inputs(seed: int = 0) -> dict:
    arg_keys = jax.random.split(jax.random.key(seed), 4)
    return {
        "raw_samples": gaussian(arg_keys[0], (INPUTS, SAMPLES), 1.0, 6.0, ((0, 32),)),
        "stack_code": draw_stack_code(jax.random.fold_in(arg_keys[3], 71), 0),
        "stack_owner": draw_stack_owner(jax.random.fold_in(arg_keys[3], 71), 0),
    }


def window_table():
    length = TAPS * FRAME
    sample = jnp.arange(length).astype(jnp.float32)
    centred = (sample - length / 2 + 0.5) / FRAME
    hanning = 0.5 - 0.5 * jnp.cos(2.0 * math.pi * (sample + 0.5) / length)
    weights = jnp.sinc(centred) * hanning
    weights = weights * jnp.sqrt(FRAME / jnp.sum(weights * weights))
    return weights.reshape(TAPS, FRAME)

def angle_of(left_index, right_index, modulus):
    product = left_index[:, None] * right_index[None, :] % modulus
    return 2.0 * math.pi * product.astype(jnp.float32) / modulus

def first_table():
    angles = angle_of(jnp.arange(FA, dtype=jnp.int32), jnp.arange(FA, dtype=jnp.int32), FA)
    return jnp.concatenate([jnp.cos(angles), -jnp.sin(angles)], axis=1).astype(jnp.bfloat16)

def twiddles():
    angles = angle_of(jnp.arange(FA, dtype=jnp.int32), jnp.arange(FB, dtype=jnp.int32), FRAME)
    return (jnp.cos(angles), jnp.sin(angles))

def second_table(second_count):
    angles = angle_of(jnp.arange(FB, dtype=jnp.int32), jnp.arange(second_count, dtype=jnp.int32), FB)
    cosine = jnp.cos(angles)
    sine_part = jnp.sin(angles)
    top_rows = jnp.stack([cosine, -sine_part], axis=1)
    low_rows = jnp.stack([sine_part, cosine], axis=1)
    return jnp.stack([top_rows, low_rows], axis=0).astype(jnp.bfloat16)

def channelize(samples, second_count):
    window = window_table()
    inputs = samples.shape[0]
    framed = samples.reshape(inputs, SPECTRA + TAPS - 1, FRAME)
    summed = jnp.zeros((inputs, SPECTRA, FRAME), jnp.float32)
    for tap_index in range(TAPS):
        summed = summed + window[tap_index] * framed[:, tap_index:tap_index + SPECTRA].astype(jnp.float32)
    frames = summed.astype(jnp.bfloat16).reshape(inputs * SPECTRA, FA, FB)
    sectioned = jnp.einsum('rab,ak->rkb', frames.astype(jnp.float32), first_table().astype(jnp.float32))
    cosine, sine_part = twiddles()
    real_part = sectioned[:, :FA]
    imag_part = sectioned[:, FA:]
    mixed = jnp.stack([real_part * cosine + imag_part * sine_part, imag_part * cosine - real_part * sine_part], axis=2)
    mixed = mixed.astype(jnp.bfloat16)
    spectra = jnp.einsum('rkpb,pbqm->rqmk', mixed.astype(jnp.float32), second_table(second_count).astype(jnp.float32))
    spectra = spectra / math.sqrt(FRAME)
    return spectra.reshape(inputs, SPECTRA, 2, second_count * FA).astype(jnp.bfloat16)

def correlate(own_block, other_block):
    left_rows = own_block.reshape(own_block.shape[0], 2 * own_block.shape[1], own_block.shape[3])
    turned = jnp.stack([-other_block[:, :, 1], other_block[:, :, 0]], axis=2)
    right_rows = jnp.stack([other_block, turned], axis=3)
    right_rows = right_rows.reshape(other_block.shape[0], 2 * other_block.shape[1], 2, other_block.shape[3])
    return jnp.einsum('ikc,jkqc->ijqc', left_rows.astype(jnp.float32), right_rows.astype(jnp.float32))

def stack_targets(code_rows, usable):
    target = jnp.where(code_rows >= 0, code_rows, -1 - code_rows)
    return jnp.where(usable, target, STACKS)

def add_pairs(totals, values, code_rows, usable):
    target = stack_targets(code_rows, usable)
    orient = jnp.where(code_rows >= 0, 1.0, -1.0).astype(jnp.float32)
    values = jnp.stack([values[:, :, 0], values[:, :, 1] * orient[:, :, None]], axis=2)
    flattened = values.reshape(-1, 2, values.shape[3])
    return totals + jax.ops.segment_sum(flattened, target.reshape(-1), num_segments=STACKS + 1)

def slot_sources(owner_ids, owners, capacity, stacks):
    member = (owner_ids[:, None] == jnp.arange(owners, dtype=jnp.int32)[None, :]).astype(jnp.int32)
    earlier = jnp.cumsum(member, axis=0) - member
    ranking = lax.optimization_barrier(jnp.sum(earlier * member, axis=1))
    slot_ids = owner_ids * capacity + ranking
    filled = jnp.full((owners * capacity,), stacks, jnp.int32)
    return filled.at[slot_ids].set(jnp.arange(stacks, dtype=jnp.int32))

def reference(raw_samples, stack_code, stack_owner):
    group_rows = min(64, INPUTS)
    groups = INPUTS // group_rows
    second_count = CHANS // FA

    def one_group(grouped):
        return channelize(grouped, second_count)
    spectra = lax.map(one_group, raw_samples.reshape(groups, group_rows, SAMPLES))
    local_ids = jnp.arange(group_rows, dtype=jnp.int32)
    empty = jnp.zeros((STACKS + 1, 2, CHANS), jnp.float32)

    def outer(totals, left_index):
        own = spectra[left_index]
        row_ids = left_index * group_rows + local_ids

        def inner(running, right_index):
            other = spectra[right_index]
            col_ids = right_index * group_rows + local_ids
            usable = col_ids[None, :] > row_ids[:, None]
            code_rows = lax.dynamic_slice(stack_code, (left_index * group_rows, right_index * group_rows), (group_rows, group_rows))
            return (add_pairs(running, correlate(own, other), code_rows, usable), None)
        return (lax.scan(inner, totals, jnp.arange(groups, dtype=jnp.int32))[0], None)
    totals = lax.scan(outer, empty, jnp.arange(groups, dtype=jnp.int32))[0]
    all_ids = jnp.arange(INPUTS, dtype=jnp.int32)
    upper = all_ids[None, :] > all_ids[:, None]
    target = stack_targets(stack_code, upper)
    counts = jax.ops.segment_sum(jnp.ones((INPUTS * INPUTS,), jnp.float32), target.reshape(-1), num_segments=STACKS + 1)
    means = totals / jnp.maximum(counts, 1.0)[:, None, None]
    means = means.at[STACKS].set(0.0)
    sources = slot_sources(stack_owner, OWNERS, CAP, STACKS)
    return means[sources]
```

```python
import functools
import math

import jax
import jax.numpy as jnp
import numpy as np
from jax import lax
from jax.experimental import pallas as pl
from jax.experimental.pallas import tpu as pltpu
from jax.sharding import PartitionSpec as P

SPECTRA = 4
TAPS = 8
FA = 64
FB = 128
FRAME = 8192
CHANS = 2048
STACKS = 382
QS = CHANS // FA
STACK_ROWS = 384
HALF_STACKS = 192
GROUP = 8
MB = 1024 * 1024


def window_table():
    length = TAPS * FRAME
    sample = np.arange(length, dtype=np.float64)
    centred = (sample - length / 2 + 0.5) / FRAME
    hanning = 0.5 - 0.5 * np.cos(2.0 * np.pi * (sample + 0.5) / length)
    weights = np.sinc(centred) * hanning
    weights = weights * np.sqrt(FRAME / np.sum(weights * weights))
    return weights.reshape(TAPS, FRAME).astype(np.float32)


def angle_of(left_count, right_count, modulus):
    product = np.arange(left_count)[:, None] * np.arange(right_count)[None, :] % modulus
    return 2.0 * np.pi * product / modulus


def first_table():
    angles = angle_of(FA, FA, FA)
    return np.concatenate([np.cos(angles), -np.sin(angles)], axis=0)


def twiddles():
    angles = angle_of(FA, FB, FRAME)
    return np.cos(angles).astype(np.float32), np.sin(angles).astype(np.float32)


def second_table(order):
    angles = angle_of(FB, QS, FB).T[np.asarray(order)]
    cosine, sine = np.cos(angles), np.sin(angles)
    real_rows = np.concatenate([cosine, sine], axis=1)
    imag_rows = np.concatenate([-sine, cosine], axis=1)
    return np.concatenate([real_rows, imag_rows], axis=0)


def channelize_kernel(
    x_ref, window_ref, first_ref, cos_ref, sin_ref, second_ref, out_ref, frames, mixed, turned
):
    inputs = x_ref.shape[0]
    for a in range(FA):
        sums = [None] * SPECTRA
        for r in range(SPECTRA + TAPS - 1):
            x = x_ref[:, r * FRAME + a * FB : r * FRAME + (a + 1) * FB].astype(jnp.float32)
            for t in range(SPECTRA):
                if 0 <= r - t < TAPS:
                    term = window_ref[r - t : r - t + 1, a * FB : (a + 1) * FB] * x
                    sums[t] = term if sums[t] is None else sums[t] + term
        for t in range(SPECTRA):
            frames[pl.ds(t * inputs * FA + a, inputs, stride=FA), :] = sums[t]
    for t in range(SPECTRA):
        rows = frames[t * inputs * FA : (t + 1) * inputs * FA, :].astype(jnp.bfloat16)
        wide = jnp.concatenate([rows[i * FA : (i + 1) * FA] for i in range(inputs)], axis=1)
        section = jnp.dot(first_ref[...], wide, preferred_element_type=jnp.float32)
        for i in range(inputs):
            real = section[:FA, i * FB : (i + 1) * FB]
            imag = section[FA:, i * FB : (i + 1) * FB]
            cosine, sine = cos_ref[...], sin_ref[...]
            twisted = jnp.concatenate(
                [real * cosine + imag * sine, imag * cosine - real * sine], axis=1
            ).astype(jnp.bfloat16)
            for h in range(2):
                start = ((i * 2 + h) * SPECTRA + t) * 32
                mixed[start : start + 32, :] = twisted[h * 32 : (h + 1) * 32]
    for i in range(inputs):
        spectra = lax.dot_general(
            second_ref[...],
            mixed[i * 256 : (i + 1) * 256, :],
            (((1,), (1,)), ((), ())),
            preferred_element_type=jnp.float32,
        ) * (1.0 / math.sqrt(FRAME))
        for m in range(2):
            for g in range(QS // 8):
                for h in range(2):
                    tile = spectra[m * QS + g * 8 : m * QS + g * 8 + 8, h * 128 : (h + 1) * 128]
                    start = ((h * 2 + m) * QS + g * 8) * inputs + i
                    turned[pl.ds(start, 8, stride=inputs), :] = tile
    for part in range(4):
        rows = turned[part * QS * inputs : (part + 1) * QS * inputs, :]
        out_ref[:, part * 128 : (part + 1) * 128] = rows.astype(jnp.bfloat16)


def channelize(samples, order):
    inputs = samples.shape[0]
    cosine, sine = twiddles()
    return pl.pallas_call(
        channelize_kernel,
        out_shape=jax.ShapeDtypeStruct((QS * inputs, 512), jnp.bfloat16),
        scratch_shapes=[
            pltpu.VMEM((SPECTRA * inputs * FA, FB), jnp.float32),
            pltpu.VMEM((SPECTRA * inputs * FA, 2 * FB), jnp.bfloat16),
            pltpu.VMEM((4 * QS * inputs, 128), jnp.float32),
        ],
        compiler_params=pltpu.CompilerParams(vmem_limit_bytes=32 * MB),
        name="channelize",
    )(
        samples,
        jnp.asarray(window_table()),
        jnp.asarray(first_table(), jnp.bfloat16),
        jnp.asarray(cosine),
        jnp.asarray(sine),
        jnp.asarray(second_table(order), jnp.bfloat16),
    )


def one_hot(stack, row):
    return jnp.where(stack == row, jnp.ones_like(stack), jnp.zeros_like(stack))


def stack_ids(inputs):
    ids = lax.broadcasted_iota(jnp.int32, (STACK_ROWS, inputs), 0) - HALF_STACKS
    return ids.astype(jnp.float32).astype(jnp.bfloat16)


def targets_kernel(padded, code_ref, owner_ref, target_ref, sign_ref, count_ref, slot_ref):
    inputs = code_ref.shape[1]
    half = inputs // 2
    row = lax.broadcasted_iota(jnp.int32, (half, inputs), 0)
    col = lax.broadcasted_iota(jnp.int32, (half, inputs), 1)
    apart = jnp.bitwise_and(col - row, inputs - 1)
    code = jnp.where((apart >= 1) & (apart <= half), code_ref[:half, :], code_ref[half:, :])
    target = jnp.where(code >= 0, code, -1 - code)
    target = jnp.where(apart == 0, STACK_ROWS, target) - HALF_STACKS
    target_ref[...] = target.astype(jnp.float32)
    sign_ref[...] = jnp.where(code >= 0, 1.0, -1.0)
    stack = stack_ids(inputs)
    ones = jnp.ones((GROUP * inputs, 128), jnp.bfloat16)
    count_ref[...] = jnp.zeros(count_ref.shape, jnp.float32)

    def step(g, carry):
        rows = target_ref[pl.ds(pl.multiple_of(g * GROUP, GROUP), GROUP), :].astype(jnp.bfloat16)
        member = jnp.concatenate([one_hot(stack, rows[u : u + 1]) for u in range(GROUP)], axis=1)
        count_ref[...] += jnp.dot(member, ones, preferred_element_type=jnp.float32)
        return carry

    lax.fori_loop(0, half // GROUP, step, 0)

    owner = owner_ref[...]
    across = jnp.broadcast_to(owner, (STACK_ROWS, STACK_ROWS))
    down = across.T
    before = lax.broadcasted_iota(jnp.int32, (STACK_ROWS, STACK_ROWS), 0)
    after = lax.broadcasted_iota(jnp.int32, (STACK_ROWS, STACK_ROWS), 1)
    earlier = jnp.where((across == down) & (before < after), 1.0, 0.0)
    rank = jnp.sum(earlier, axis=0, keepdims=True)
    slot_ref[...] = jnp.where(owner >= 0, owner * padded, -1.0) + rank


def targets(codes, owner, padded):
    inputs = codes.shape[1]
    return pl.pallas_call(
        functools.partial(targets_kernel, padded),
        out_shape=(
            jax.ShapeDtypeStruct((inputs // 2, inputs), jnp.float32),
            jax.ShapeDtypeStruct((inputs // 2, inputs), jnp.float32),
            jax.ShapeDtypeStruct((STACK_ROWS, 128), jnp.float32),
            jax.ShapeDtypeStruct((1, STACK_ROWS), jnp.float32),
        ),
        compiler_params=pltpu.CompilerParams(vmem_limit_bytes=32 * MB),
        name="targets",
    )(codes, owner)


def stack_kernel(
    spectra_ref, target_ref, sign_ref, count_ref, slot_ref, out_ref, wide, other, acc
):
    inputs, lanes = spectra_ref.shape
    half, blocks = inputs // 2, lanes // 256
    wide[...] = spectra_ref[...].astype(jnp.float32)
    for b in range(blocks):
        other[b * 256 : (b + 1) * 256, :] = spectra_ref[:, b * 256 : (b + 1) * 256].T
    acc[...] = jnp.zeros(acc.shape, jnp.float32)
    diagonal = lax.broadcasted_iota(jnp.int32, (32, 128), 0) == jnp.bitwise_and(
        lax.broadcasted_iota(jnp.int32, (32, 128), 1), 31
    )
    diagonal = jnp.where(diagonal, 1.0, 0.0)
    stack = stack_ids(inputs)

    def spread(rows):
        parts = []
        for u in range(GROUP):
            real = diagonal * rows[u : u + 1, :128]
            imag = diagonal * rows[u : u + 1, 128:]
            parts.append(jnp.concatenate([real, imag], axis=1))
            parts.append(jnp.concatenate([imag, -real], axis=1))
        return jnp.concatenate(parts, axis=0).astype(jnp.bfloat16)

    def step(g, carry):
        start = pl.multiple_of(g * GROUP, GROUP)
        products = []
        for b in range(blocks):
            right = other[b * 256 : (b + 1) * 256, :]
            products.append(
                [
                    jnp.dot(
                        spread(wide[pl.ds(start + p * half, GROUP), b * 256 : (b + 1) * 256]),
                        right,
                        preferred_element_type=jnp.float32,
                    )
                    for p in range(2)
                ]
            )
        row = lax.broadcasted_iota(jnp.int32, (GROUP, inputs), 0) + start
        col = lax.broadcasted_iota(jnp.int32, (GROUP, inputs), 1)
        apart = jnp.bitwise_and(col - row, inputs - 1)
        first = jnp.where((apart >= 1) & (apart <= half), 1.0, 0.0)
        signs = sign_ref[pl.ds(start, GROUP), :]
        goal = target_ref[pl.ds(start, GROUP), :].astype(jnp.bfloat16)
        values, members = [], []
        for u in range(GROUP):
            use = jnp.broadcast_to(first[u : u + 1], (32, inputs)) > 0.5
            sign = signs[u : u + 1]
            reals, imags = [], []
            for b in range(blocks):
                low, high = products[b]
                reals.append(
                    jnp.where(use, low[u * 64 : u * 64 + 32], high[u * 64 : u * 64 + 32])
                )
                imags.append(
                    sign
                    * jnp.where(use, low[u * 64 + 32 : u * 64 + 64], high[u * 64 + 32 : u * 64 + 64])
                )
            values.append(jnp.concatenate(reals + imags, axis=0).astype(jnp.bfloat16))
            members.append(one_hot(stack, goal[u : u + 1]))
        acc[...] += lax.dot_general(
            jnp.concatenate(members, axis=1),
            jnp.concatenate(values, axis=1),
            (((1,), (1,)), ((), ())),
            preferred_element_type=jnp.float32,
        )
        return carry

    lax.fori_loop(0, half // GROUP, step, 0)
    width = acc.shape[1]
    means = (acc[...] / jnp.maximum(count_ref[:, :width], 1.0)).astype(jnp.bfloat16)
    slots = out_ref.shape[0]
    slot_id = lax.broadcasted_iota(jnp.int32, (slots, STACK_ROWS), 0).astype(jnp.float32)
    place = jnp.where(slot_id == slot_ref[...], 1.0, 0.0).astype(jnp.bfloat16)
    out_ref[...] = jnp.dot(place, means, preferred_element_type=jnp.float32).astype(jnp.bfloat16)


def stack_means(spectra, target, sign, counts, slot, slots):
    inputs, lanes = spectra.shape
    width = lanes // SPECTRA
    return pl.pallas_call(
        stack_kernel,
        out_shape=jax.ShapeDtypeStruct((slots, width), jnp.bfloat16),
        scratch_shapes=[
            pltpu.VMEM((inputs, lanes), jnp.float32),
            pltpu.VMEM((lanes, inputs), jnp.bfloat16),
            pltpu.VMEM((STACK_ROWS, width), jnp.float32),
        ],
        compiler_params=pltpu.CompilerParams(vmem_limit_bytes=48 * MB),
        name="stack_means",
    )(spectra, target, sign, counts, slot)


def per_device(raw_samples, stack_code, stack_owner):
    feeds, chans = lax.axis_size("feed"), lax.axis_size("chan")
    inputs = raw_samples.shape[0]
    everyone = ("feed", "chan")
    share = CHANS // (feeds * chans)
    capacity = 2 * STACKS // feeds
    padded = -(-capacity // 16) * 16
    direct = share == FA and inputs == 8

    codes = lax.all_gather(stack_code, "feed", axis=0, tiled=True)
    owner = jnp.pad(
        stack_owner.astype(jnp.float32), (0, STACK_ROWS - STACKS), constant_values=-1.0
    )
    target, sign, counts, slot = targets(codes, owner.reshape(1, STACK_ROWS), padded)

    if direct:
        order = [c * feeds + f for f in range(feeds) for c in range(chans)]
        local = channelize(raw_samples, order).reshape(feeds * chans, inputs, 512)
    else:
        samples = jnp.pad(raw_samples, ((0, -inputs % 8), (0, 0)))
        local = channelize(samples, list(range(QS)))
        local = local.reshape(QS, samples.shape[0], 2, 2, SPECTRA, 32)[:, :inputs]
        local = local.transpose(0, 2, 5, 1, 3, 4).reshape(chans, feeds, share, inputs, 2, SPECTRA)
        local = local.transpose(1, 0, 3, 4, 5, 2).reshape(feeds * chans, inputs, 8 * share)
    moved = lax.all_to_all(local, everyone, split_axis=0, concat_axis=0, tiled=True)
    if not direct:
        moved = moved.reshape(feeds * chans, inputs, 8, share)
        moved = jnp.pad(moved, ((0, 0), (0, 0), (0, 0), (0, 32 - share)))
    moved = moved.reshape(feeds * chans * inputs, -1)

    means = stack_means(moved, target, sign, counts, slot, feeds * padded)
    means = means.reshape(feeds, padded, -1)
    landed = lax.all_to_all(means, "feed", split_axis=0, concat_axis=0, tiled=True)
    landed = landed[:, :capacity].reshape(feeds, capacity, 2, -1)[..., :share]
    return landed.transpose(1, 2, 0, 3).reshape(capacity, 2, feeds * share).astype(jnp.float32)


def solution(mesh):
    placed = (P(("feed", "chan"), None), P("feed", None), P())
    return jax.shard_map(
        per_device, mesh=mesh, in_specs=placed, out_specs=P("feed", None, "chan"), check_vma=False
    )
```

```python
import functools
import math

import jax
import jax.numpy as jnp
import numpy as np
from jax import lax
from jax.experimental import pallas as pl
from jax.experimental.pallas import tpu as pltpu
from jax.sharding import PartitionSpec as P

SPECTRA = 4
TAPS = 8
FA = 64
FB = 128
FRAME = 8192
CHANS = 2048
STACKS = 382
QS = CHANS // FA
STACK_ROWS = 384
HALF_STACKS = 192
GROUP = 16
PIECES = 2
CODE_BASE = 384
MB = 1024 * 1024


def window_table():
    length = TAPS * FRAME
    sample = np.arange(length, dtype=np.float64)
    centred = (sample - length / 2 + 0.5) / FRAME
    hanning = 0.5 - 0.5 * np.cos(2.0 * np.pi * (sample + 0.5) / length)
    weights = np.sinc(centred) * hanning
    weights = weights * np.sqrt(FRAME / np.sum(weights * weights))
    return weights.reshape(TAPS, FRAME).astype(np.float32)


def angle_of(left_count, right_count, modulus):
    product = np.arange(left_count)[:, None] * np.arange(right_count)[None, :] % modulus
    return 2.0 * np.pi * product / modulus


def first_table():
    angles = angle_of(FA, FA, FA)
    return np.concatenate([np.cos(angles), -np.sin(angles)], axis=0)


def twiddles():
    angles = angle_of(FA, FB, FRAME)
    return np.cos(angles).astype(np.float32), np.sin(angles).astype(np.float32)


def second_table(order):
    angles = angle_of(FB, QS, FB).T[np.asarray(order)]
    cosine, sine = np.cos(angles), np.sin(angles)
    real_rows = np.concatenate([cosine, sine], axis=1)
    imag_rows = np.concatenate([-sine, cosine], axis=1)
    return np.concatenate([real_rows, imag_rows], axis=0)


def channelize_kernel(
    direct, x_hbm, code_hbm, window_hbm, first_hbm, cos_hbm, sin_hbm, second_hbm, out_ref,
    x_ref, code_ref, window_ref, first_ref, cos_ref, sin_ref, second_ref, frames, mixed, turned,
    x_sems, sems,
):
    inputs = x_ref.shape[0]
    piece = FRAME // PIECES
    pieces = []
    for k in range(PIECES):
        window_copy = pltpu.make_async_copy(
            window_hbm.at[:, k * piece : (k + 1) * piece],
            window_ref.at[:, k * piece : (k + 1) * piece],
            x_sems.at[k, 0],
        )
        window_copy.start()
        copies = [window_copy]
        for r in range(SPECTRA + TAPS - 1):
            at = slice(r * FRAME + k * piece, r * FRAME + (k + 1) * piece)
            copy = pltpu.make_async_copy(x_hbm.at[:, at], x_ref.at[:, at], x_sems.at[k, 1 + r])
            copy.start()
            copies.append(copy)
        pieces.append(copies)
    others = []
    for n, (source, target) in enumerate(
        [
            (code_hbm, code_ref),
            (first_hbm, first_ref),
            (cos_hbm, cos_ref),
            (sin_hbm, sin_ref),
            (second_hbm, second_ref),
        ]
    ):
        copy = pltpu.make_async_copy(source, target, sems.at[n])
        copy.start()
        others.append(copy)

    for a in range(FA):
        if a % (FA // PIECES) == 0:
            for copy in pieces[a // (FA // PIECES)]:
                copy.wait()
        sums = [None] * SPECTRA
        for r in range(SPECTRA + TAPS - 1):
            x = x_ref[:, r * FRAME + a * FB : r * FRAME + (a + 1) * FB].astype(jnp.float32)
            for t in range(SPECTRA):
                if 0 <= r - t < TAPS:
                    term = window_ref[r - t : r - t + 1, a * FB : (a + 1) * FB] * x
                    sums[t] = term if sums[t] is None else sums[t] + term
        for t in range(SPECTRA):
            frames[pl.ds(t * inputs * FA + a, inputs, stride=FA), :] = sums[t]
    for copy in others:
        copy.wait()

    count = code_ref.shape[1]
    half = count // 2
    place = lax.axis_index("feed") * lax.axis_size("chan") + lax.axis_index("chan")
    if direct:
        start = pl.multiple_of(lax.axis_index("chan") * inputs, 8)
        codes = code_ref[pl.ds(start, inputs), :]
        first_input = place * inputs
    else:
        codes = code_ref[...]
        first_input = place * (count // (lax.axis_size("feed") * lax.axis_size("chan")))
    row = lax.broadcasted_iota(jnp.int32, (inputs, half), 0) + first_input
    col = lax.broadcasted_iota(jnp.int32, (inputs, half), 1)
    apart = jnp.bitwise_and(col - row, count - 1)
    code = jnp.where((apart >= 1) & (apart <= half), codes[:, :half], codes[:, half:])
    shifted = code + CODE_BASE
    code = jnp.left_shift(128 + jnp.bitwise_and(shifted, 127), jnp.right_shift(shifted, 7))
    code = code.astype(jnp.float32)
    out_ref[:, 512:] = jnp.concatenate([code] * QS, axis=0).astype(jnp.bfloat16)

    for t in range(SPECTRA):
        rows = frames[t * inputs * FA : (t + 1) * inputs * FA, :].astype(jnp.bfloat16)
        wide = jnp.concatenate([rows[i * FA : (i + 1) * FA] for i in range(inputs)], axis=1)
        section = jnp.dot(first_ref[...], wide, preferred_element_type=jnp.float32)
        for i in range(inputs):
            real = section[:FA, i * FB : (i + 1) * FB]
            imag = section[FA:, i * FB : (i + 1) * FB]
            cosine, sine = cos_ref[...], sin_ref[...]
            twisted = jnp.concatenate(
                [real * cosine + imag * sine, imag * cosine - real * sine], axis=1
            ).astype(jnp.bfloat16)
            for h in range(2):
                start = ((i * 2 + h) * SPECTRA + t) * 32
                mixed[start : start + 32, :] = twisted[h * 32 : (h + 1) * 32]
    for i in range(inputs):
        spectra = lax.dot_general(
            second_ref[...],
            mixed[i * 256 : (i + 1) * 256, :],
            (((1,), (1,)), ((), ())),
            preferred_element_type=jnp.float32,
        ) * (1.0 / math.sqrt(FRAME))
        for m in range(2):
            for g in range(QS // 8):
                for h in range(2):
                    tile = spectra[m * QS + g * 8 : m * QS + g * 8 + 8, h * 128 : (h + 1) * 128]
                    start = ((h * 2 + m) * QS + g * 8) * inputs + i
                    turned[pl.ds(start, 8, stride=inputs), :] = tile
    for part in range(4):
        rows = turned[part * QS * inputs : (part + 1) * QS * inputs, :]
        out_ref[:, part * 128 : (part + 1) * 128] = rows.astype(jnp.bfloat16)


def channelize(samples, codes, order, direct):
    inputs = samples.shape[0]
    cosine, sine = twiddles()
    operands = (
        samples,
        codes,
        jnp.asarray(window_table()),
        jnp.asarray(first_table(), jnp.bfloat16),
        jnp.asarray(cosine),
        jnp.asarray(sine),
        jnp.asarray(second_table(order), jnp.bfloat16),
    )
    return pl.pallas_call(
        functools.partial(channelize_kernel, direct),
        out_shape=jax.ShapeDtypeStruct((QS * inputs, 512 + codes.shape[1] // 2), jnp.bfloat16),
        in_specs=[pl.BlockSpec(memory_space=pl.ANY)] * len(operands),
        scratch_shapes=[pltpu.VMEM(value.shape, value.dtype) for value in operands]
        + [
            pltpu.VMEM((SPECTRA * inputs * FA, FB), jnp.float32),
            pltpu.VMEM((SPECTRA * inputs * FA, 2 * FB), jnp.bfloat16),
            pltpu.VMEM((4 * QS * inputs, 128), jnp.float32),
            pltpu.SemaphoreType.DMA((PIECES, SPECTRA + TAPS)),
            pltpu.SemaphoreType.DMA((5,)),
        ],
        compiler_params=pltpu.CompilerParams(vmem_limit_bytes=56 * MB),
        name="channelize",
    )(*operands)


def stack_kernel(
    padded, data_ref, owner_ref, out_ref, wide, other, goal_ref, mask_ref, held, acc, tally
):
    inputs = data_ref.shape[0]
    half = inputs // 2
    lanes = data_ref.shape[1] - half
    blocks = lanes // 256
    width = lanes // SPECTRA
    steps = half // GROUP

    value = data_ref[:, lanes:].astype(jnp.float32).astype(jnp.int32)
    power = jnp.zeros(value.shape, jnp.int32)
    for e in range(1, 6):
        power = power + jnp.where(value >= 128 << e, 1, 0)
    code = power * 128 + jnp.right_shift(value, power) - 128 - CODE_BASE
    row = lax.broadcasted_iota(jnp.int32, (half, half), 0)
    col = lax.broadcasted_iota(jnp.int32, (half, half), 1)
    ahead = col > row
    low, high = code[:half], code[half:]
    code = jnp.concatenate([jnp.where(ahead, low, high), jnp.where(ahead, high, low)], axis=1)
    target = jnp.where(code >= 0, code, -1 - code)
    row = lax.broadcasted_iota(jnp.int32, (half, inputs), 0)
    col = lax.broadcasted_iota(jnp.int32, (half, inputs), 1)
    upper = target >= HALF_STACKS
    used = col != row
    goal_ref[...] = jnp.where(upper, target - HALF_STACKS, target).astype(jnp.float32)
    left = jnp.where(used & ~upper, 1.0, 0.0)
    right = jnp.where(used & upper, 1.0, 0.0)
    sign = jnp.where(code >= 0, 1.0, -1.0)
    for n, mask in enumerate((left, right, left * sign, right * sign)):
        mask_ref[n] = mask

    wide[...] = data_ref[:, :lanes].astype(jnp.float32)
    for b in range(blocks):
        other[b * 256 : (b + 1) * 256, :] = data_ref[:, b * 256 : (b + 1) * 256].T
    acc[...] = jnp.zeros(acc.shape, jnp.float32)
    tally[...] = jnp.zeros(tally.shape, jnp.float32)
    diagonal = lax.broadcasted_iota(jnp.int32, (32, 128), 0) == jnp.bitwise_and(
        lax.broadcasted_iota(jnp.int32, (32, 128), 1), 31
    )
    diagonal = jnp.where(diagonal, 1.0, 0.0)
    stack = lax.broadcasted_iota(jnp.int32, (HALF_STACKS, inputs), 0)
    stack = stack.astype(jnp.float32).astype(jnp.bfloat16)

    def spread(rows):
        parts = []
        for u in range(rows.shape[0]):
            real = diagonal * rows[u : u + 1, :128]
            imag = diagonal * rows[u : u + 1, 128:]
            parts.append(jnp.concatenate([real, imag], axis=1))
            parts.append(jnp.concatenate([imag, -real], axis=1))
        return jnp.concatenate(parts, axis=0).astype(jnp.bfloat16)

    def multiply(g):
        start = g * GROUP
        if not isinstance(g, int):
            start = pl.multiple_of(start, GROUP)
        row = lax.broadcasted_iota(jnp.int32, (GROUP, inputs), 0) + start
        col = lax.broadcasted_iota(jnp.int32, (GROUP, inputs), 1)
        apart = jnp.bitwise_and(col - row, inputs - 1)
        first = jnp.where((apart >= 1) & (apart <= half), 1.0, 0.0)
        for b in range(blocks):
            low = wide[pl.ds(start, GROUP), b * 256 : (b + 1) * 256]
            high = wide[pl.ds(start + half, GROUP), b * 256 : (b + 1) * 256]
            rows = [x[u : u + 1] for u in range(GROUP) for x in (low, high)]
            product = jnp.dot(
                spread(jnp.concatenate(rows, axis=0)),
                other[b * 256 : (b + 1) * 256, :],
                preferred_element_type=jnp.float32,
            )
            for u in range(GROUP):
                use = jnp.broadcast_to(first[u : u + 1], (64, inputs)) > 0.5
                at = u * 128
                chosen = jnp.where(use, product[at : at + 64], product[at + 64 : at + 128])
                chosen = chosen.astype(jnp.bfloat16)
                columns = slice(u * inputs, (u + 1) * inputs)
                held[b * 32 : b * 32 + 32, columns] = chosen[:32]
                at = (blocks + b) * 32
                held[at : at + 32, columns] = chosen[32:]

    def accumulate(g):
        start = g * GROUP
        if not isinstance(g, int):
            start = pl.multiple_of(start, GROUP)
        goal = goal_ref[pl.ds(start, GROUP), :].astype(jnp.bfloat16)
        masks = [mask_ref[n, pl.ds(start, GROUP), :].astype(jnp.bfloat16) for n in range(4)]
        members, values = [], []
        lefts = rights = None
        for u in range(GROUP):
            columns = slice(u * inputs, (u + 1) * inputs)
            left, right, left_sign, right_sign = [mask[u : u + 1] for mask in masks]
            real = held[: width // 2, columns]
            imag = held[width // 2 :, columns]
            values.append(
                jnp.concatenate(
                    [real * left, imag * left_sign, real * right, imag * right_sign], axis=0
                )
            )
            member = jnp.where(
                stack == goal[u : u + 1], jnp.ones_like(stack), jnp.zeros_like(stack)
            )
            members.append(member)
            lefts = member * left if lefts is None else lefts + member * left
            rights = member * right if rights is None else rights + member * right
        acc[...] += lax.dot_general(
            jnp.concatenate(members, axis=1),
            jnp.concatenate(values, axis=1),
            (((1,), (1,)), ((), ())),
            preferred_element_type=jnp.float32,
        )
        tally[0] += lefts.astype(jnp.float32)
        tally[1] += rights.astype(jnp.float32)

    def step(g, carry):
        accumulate(g)
        multiply(g + 1)
        return carry

    multiply(0)
    lax.fori_loop(0, steps - 1, step, 0)
    accumulate(steps - 1)

    owner = owner_ref[...]
    across = jnp.broadcast_to(owner, (STACK_ROWS, STACK_ROWS))
    down = across.T
    before = lax.broadcasted_iota(jnp.int32, (STACK_ROWS, STACK_ROWS), 0)
    after = lax.broadcasted_iota(jnp.int32, (STACK_ROWS, STACK_ROWS), 1)
    earlier = jnp.where((across == down) & (before < after), 1.0, 0.0)
    rank = jnp.sum(earlier, axis=0, keepdims=True)
    slot = jnp.where(owner >= 0, owner * padded, -STACK_ROWS) + rank

    means = []
    for n in range(2):
        counts = jnp.maximum(jnp.sum(tally[n], axis=1, keepdims=True), 1.0)
        means.append((acc[:, n * width : (n + 1) * width] / counts).astype(jnp.bfloat16))
    means = jnp.concatenate(means, axis=0)
    slots = out_ref.shape[0]
    slot_id = lax.broadcasted_iota(jnp.int32, (slots, STACK_ROWS), 0).astype(jnp.float32)
    place = jnp.where(slot_id == slot, 1.0, 0.0).astype(jnp.bfloat16)
    out_ref[...] = jnp.dot(place, means, preferred_element_type=jnp.float32).astype(jnp.bfloat16)


def stack_means(data, owner, padded, feeds):
    inputs = data.shape[0]
    half = inputs // 2
    lanes = data.shape[1] - half
    width = lanes // SPECTRA
    return pl.pallas_call(
        functools.partial(stack_kernel, padded),
        out_shape=jax.ShapeDtypeStruct((feeds * padded, width), jnp.bfloat16),
        scratch_shapes=[
            pltpu.VMEM((inputs, lanes), jnp.float32),
            pltpu.VMEM((lanes, inputs), jnp.bfloat16),
            pltpu.VMEM((half, inputs), jnp.float32),
            pltpu.VMEM((4, half, inputs), jnp.float32),
            pltpu.VMEM((width, GROUP * inputs), jnp.bfloat16),
            pltpu.VMEM((HALF_STACKS, 2 * width), jnp.float32),
            pltpu.VMEM((2, HALF_STACKS, inputs), jnp.float32),
        ],
        compiler_params=pltpu.CompilerParams(vmem_limit_bytes=48 * MB),
        name="stack_means",
    )(data, owner)


def lay_out_kernel(feeds, padded, capacity, landed_ref, out_ref):
    lane = lax.broadcasted_iota(jnp.int32, (padded, 128), 1)
    for pair in range(feeds // 2):
        left = landed_ref[2 * pair * padded : (2 * pair + 1) * padded, :].astype(jnp.float32)
        right = landed_ref[(2 * pair + 1) * padded : (2 * pair + 2) * padded, :].astype(
            jnp.float32
        )
        real = jnp.where(lane < 64, left, pltpu.roll(right, 64, 1))
        imag = jnp.where(lane < 64, pltpu.roll(left, 64, 1), right)
        for part, value in enumerate((real, imag)):
            out_ref[pl.ds(pair * 2 + part, capacity, stride=feeds), :] = value[:capacity]


def lay_out(landed, feeds, padded, capacity):
    return pl.pallas_call(
        functools.partial(lay_out_kernel, feeds, padded, capacity),
        out_shape=jax.ShapeDtypeStruct((capacity * feeds, 128), jnp.float32),
        compiler_params=pltpu.CompilerParams(vmem_limit_bytes=32 * MB),
        name="lay_out",
    )(landed)


def per_device(raw_samples, stack_code, stack_owner):
    feeds, chans = lax.axis_size("feed"), lax.axis_size("chan")
    devices = feeds * chans
    inputs = raw_samples.shape[0]
    half = stack_code.shape[1] // 2
    everyone = ("feed", "chan")
    share = CHANS // devices
    capacity = 2 * STACKS // feeds
    padded = -(-capacity // 16) * 16
    direct = share == FA and inputs == 8

    owner = jnp.pad(
        stack_owner.astype(jnp.float32), (0, STACK_ROWS - STACKS), constant_values=-1.0
    ).reshape(1, STACK_ROWS)

    if direct:
        order = [c * feeds + f for f in range(feeds) for c in range(chans)]
        local = channelize(raw_samples, stack_code, order, True)
        local = local.reshape(devices, inputs, -1)
    else:
        samples = jnp.pad(raw_samples, ((0, -inputs % 8), (0, 0)))
        codes = lax.dynamic_slice_in_dim(stack_code, lax.axis_index("chan") * inputs, inputs)
        codes = jnp.pad(codes, ((0, -inputs % 8), (0, 0)))
        local = channelize(samples, codes, list(range(QS)), False)
        local = local.reshape(QS, samples.shape[0], -1)[:, :inputs]
        codes = jnp.broadcast_to(local[:1, :, 512:], (devices, inputs, half))
        local = local[:, :, :512].reshape(QS, inputs, 2, 2, SPECTRA, 32)
        local = local.transpose(0, 2, 5, 1, 3, 4).reshape(chans, feeds, share, inputs, 2, SPECTRA)
        local = local.transpose(1, 0, 3, 4, 5, 2).reshape(devices, inputs, 8 * share)
        local = jnp.concatenate([local, codes], axis=2)
    moved = lax.all_to_all(local, everyone, split_axis=0, concat_axis=0, tiled=True)
    if not direct:
        codes = moved[:, :, 8 * share :]
        moved = moved[:, :, : 8 * share].reshape(devices, inputs, 8, share)
        moved = jnp.pad(moved, ((0, 0), (0, 0), (0, 0), (0, 32 - share)))
        moved = jnp.concatenate([moved.reshape(devices, inputs, 256), codes], axis=2)
    moved = moved.reshape(devices * inputs, -1)

    means = stack_means(moved, owner, padded, feeds)
    means = means.reshape(feeds, padded, -1)
    landed = lax.all_to_all(means, "feed", split_axis=0, concat_axis=0, tiled=True)
    if direct:
        landed = lay_out(landed.reshape(feeds * padded, -1), feeds, padded, capacity)
        landed = landed.reshape(capacity, feeds // 2, 2, 128).transpose(0, 2, 1, 3)
        return landed.reshape(capacity, 2, feeds * share)
    landed = landed[:, :capacity].reshape(feeds, capacity, 2, -1)[..., :share]
    return landed.transpose(1, 2, 0, 3).reshape(capacity, 2, feeds * share).astype(jnp.float32)


def solution(mesh):
    placed = (P(("feed", "chan"), None), P("feed", None), P())
    return jax.shard_map(
        per_device, mesh=mesh, in_specs=placed, out_specs=P("feed", None, "chan"), check_vma=False
    )
```

```python
import functools
import math

import jax
import jax.numpy as jnp
import numpy as np
from jax import lax
from jax.experimental import pallas as pl
from jax.experimental.pallas import tpu as pltpu
from jax.sharding import PartitionSpec as P

SPECTRA = 4
TAPS = 8
FA = 64
FB = 128
FRAME = 8192
CHANS = 2048
STACKS = 382
QS = CHANS // FA
STACK_ROWS = 384
HALF_STACKS = 192
GROUP = 16
PIECES = 2
PARTS = (slice(0, GROUP),)
CODE_BASE = 384
MB = 1024 * 1024


def window_table():
    length = TAPS * FRAME
    sample = np.arange(length, dtype=np.float64)
    centred = (sample - length / 2 + 0.5) / FRAME
    hanning = 0.5 - 0.5 * np.cos(2.0 * np.pi * (sample + 0.5) / length)
    weights = np.sinc(centred) * hanning
    weights = weights * np.sqrt(FRAME / np.sum(weights * weights))
    return weights.reshape(TAPS, FRAME).astype(np.float32)


def angle_of(left_count, right_count, modulus):
    product = np.arange(left_count)[:, None] * np.arange(right_count)[None, :] % modulus
    return 2.0 * np.pi * product / modulus


def first_table():
    angles = angle_of(FA, FA, FA)
    return np.concatenate([np.cos(angles), -np.sin(angles)], axis=0)


def twiddles():
    angles = angle_of(FA, FB, FRAME)
    return np.cos(angles).astype(np.float32), np.sin(angles).astype(np.float32)


def second_table(order):
    angles = angle_of(FB, QS, FB).T[np.asarray(order)]
    cosine, sine = np.cos(angles), np.sin(angles)
    real_rows = np.concatenate([cosine, sine], axis=1)
    imag_rows = np.concatenate([-sine, cosine], axis=1)
    return np.concatenate([real_rows, imag_rows], axis=0)


def channelize_kernel(
    direct, x_hbm, code_hbm, window_hbm, first_hbm, cos_hbm, sin_hbm, second_hbm, out_ref,
    x_ref, code_ref, window_ref, first_ref, cos_ref, sin_ref, second_ref, frames, mixed, turned,
    x_sems, sems,
):
    inputs = x_ref.shape[0]
    piece = FRAME // PIECES
    pieces = []
    for k in range(PIECES):
        window_copy = pltpu.make_async_copy(
            window_hbm.at[:, k * piece : (k + 1) * piece],
            window_ref.at[:, k * piece : (k + 1) * piece],
            x_sems.at[k, 0],
        )
        window_copy.start()
        copies = [window_copy]
        for r in range(SPECTRA + TAPS - 1):
            at = slice(r * FRAME + k * piece, r * FRAME + (k + 1) * piece)
            copy = pltpu.make_async_copy(x_hbm.at[:, at], x_ref.at[:, at], x_sems.at[k, 1 + r])
            copy.start()
            copies.append(copy)
        pieces.append(copies)
    others = []
    for n, (source, target) in enumerate(
        [
            (code_hbm, code_ref),
            (first_hbm, first_ref),
            (cos_hbm, cos_ref),
            (sin_hbm, sin_ref),
            (second_hbm, second_ref),
        ]
    ):
        copy = pltpu.make_async_copy(source, target, sems.at[n])
        copy.start()
        others.append(copy)

    for a in range(FA):
        if a % (FA // PIECES) == 0:
            for copy in pieces[a // (FA // PIECES)]:
                copy.wait()
        sums = [None] * SPECTRA
        for r in range(SPECTRA + TAPS - 1):
            x = x_ref[:, r * FRAME + a * FB : r * FRAME + (a + 1) * FB].astype(jnp.float32)
            for t in range(SPECTRA):
                if 0 <= r - t < TAPS:
                    term = window_ref[r - t : r - t + 1, a * FB : (a + 1) * FB] * x
                    sums[t] = term if sums[t] is None else sums[t] + term
        for t in range(SPECTRA):
            frames[(t * FA + a) * inputs : (t * FA + a + 1) * inputs, :] = sums[t]
    for copy in others:
        copy.wait()

    count = code_ref.shape[1]
    half = count // 2
    place = lax.axis_index("feed") * lax.axis_size("chan") + lax.axis_index("chan")
    if direct:
        start = pl.multiple_of(lax.axis_index("chan") * inputs, 8)
        codes = code_ref[pl.ds(start, inputs), :]
        first_input = place * inputs
    else:
        codes = code_ref[...]
        first_input = place * (count // (lax.axis_size("feed") * lax.axis_size("chan")))
    row = lax.broadcasted_iota(jnp.int32, (inputs, half), 0) + first_input
    col = lax.broadcasted_iota(jnp.int32, (inputs, half), 1)
    apart = jnp.bitwise_and(col - row, count - 1)
    code = jnp.where((apart >= 1) & (apart <= half), codes[:, :half], codes[:, half:])
    shifted = code + CODE_BASE
    code = jnp.left_shift(128 + jnp.bitwise_and(shifted, 127), jnp.right_shift(shifted, 7))
    code = code.astype(jnp.float32)
    out_ref[:, 512:] = jnp.concatenate([code] * QS, axis=0).astype(jnp.bfloat16)

    for t in range(SPECTRA):
        wide = [frames[pl.ds(t * FA * inputs + i, FA, stride=inputs), :] for i in range(inputs)]
        wide = jnp.concatenate([part.astype(jnp.bfloat16) for part in wide], axis=1)
        section = jnp.dot(first_ref[...], wide, preferred_element_type=jnp.float32)
        for i in range(inputs):
            real = section[:FA, i * FB : (i + 1) * FB]
            imag = section[FA:, i * FB : (i + 1) * FB]
            cosine, sine = cos_ref[...], sin_ref[...]
            twisted = jnp.concatenate(
                [real * cosine + imag * sine, imag * cosine - real * sine], axis=1
            ).astype(jnp.bfloat16)
            for part in range(4):
                start = (i * 4 + part) * 64 + t * 16
                mixed[start : start + 16, :] = twisted[part * 16 : (part + 1) * 16]
    for i in range(inputs):
        spectra = lax.dot_general(
            second_ref[...],
            mixed[i * 256 : (i + 1) * 256, :],
            (((1,), (1,)), ((), ())),
            preferred_element_type=jnp.float32,
        ) * (1.0 / math.sqrt(FRAME))
        for m in range(2):
            for g in range(QS // 8):
                for h in range(2):
                    tile = spectra[m * QS + g * 8 : m * QS + g * 8 + 8, h * 128 : (h + 1) * 128]
                    start = ((h * 2 + m) * QS + g * 8) * inputs + i
                    turned[pl.ds(start, 8, stride=inputs), :] = tile
    for part in range(4):
        rows = turned[part * QS * inputs : (part + 1) * QS * inputs, :]
        out_ref[:, part * 128 : (part + 1) * 128] = rows.astype(jnp.bfloat16)


def channelize(samples, codes, order, direct):
    inputs = samples.shape[0]
    cosine, sine = twiddles()
    operands = (
        samples,
        codes,
        jnp.asarray(window_table()),
        jnp.asarray(first_table(), jnp.bfloat16),
        jnp.asarray(cosine),
        jnp.asarray(sine),
        jnp.asarray(second_table(order), jnp.bfloat16),
    )
    return pl.pallas_call(
        functools.partial(channelize_kernel, direct),
        out_shape=jax.ShapeDtypeStruct((QS * inputs, 512 + codes.shape[1] // 2), jnp.bfloat16),
        in_specs=[pl.BlockSpec(memory_space=pl.ANY)] * len(operands),
        scratch_shapes=[pltpu.VMEM(value.shape, value.dtype) for value in operands]
        + [
            pltpu.VMEM((SPECTRA * inputs * FA, FB), jnp.float32),
            pltpu.VMEM((SPECTRA * inputs * FA, 2 * FB), jnp.bfloat16),
            pltpu.VMEM((4 * QS * inputs, 128), jnp.float32),
            pltpu.SemaphoreType.DMA((PIECES, SPECTRA + TAPS)),
            pltpu.SemaphoreType.DMA((5,)),
        ],
        compiler_params=pltpu.CompilerParams(vmem_limit_bytes=56 * MB),
        name="channelize",
    )(*operands)


def place_kernel(padded, owner_ref, place_ref):
    owner = owner_ref[...]
    across = jnp.broadcast_to(owner, (STACK_ROWS, STACK_ROWS))
    down = across.T
    before = lax.broadcasted_iota(jnp.int32, (STACK_ROWS, STACK_ROWS), 0)
    after = lax.broadcasted_iota(jnp.int32, (STACK_ROWS, STACK_ROWS), 1)
    earlier = jnp.where((across == down) & (before < after), 1.0, 0.0)
    rank = jnp.sum(earlier, axis=0, keepdims=True)
    slot = jnp.where(owner >= 0, owner * padded, -STACK_ROWS) + rank
    slot_id = lax.broadcasted_iota(jnp.int32, place_ref.shape, 0).astype(jnp.float32)
    place_ref[...] = jnp.where(slot_id == slot, 1.0, 0.0).astype(jnp.bfloat16)


def place_stacks(owner, padded, feeds):
    return pl.pallas_call(
        functools.partial(place_kernel, padded),
        out_shape=jax.ShapeDtypeStruct((feeds * padded, STACK_ROWS), jnp.bfloat16),
        compiler_params=pltpu.CompilerParams(vmem_limit_bytes=16 * MB),
        name="place_stacks",
    )(owner)


def stack_kernel(
    data_ref, place_ref, out_ref, wide, pairs, other, twin, goal_ref, mask_ref, held, acc, tally
):
    inputs = data_ref.shape[0]
    half = inputs // 2
    lanes = data_ref.shape[1] - half
    blocks = lanes // 256
    width = lanes // SPECTRA
    steps = half // GROUP

    value = data_ref[:, lanes:].astype(jnp.float32).astype(jnp.int32)
    power = jnp.zeros(value.shape, jnp.int32)
    for e in range(1, 6):
        power = power + jnp.where(value >= 128 << e, 1, 0)
    code = power * 128 + jnp.right_shift(value, power) - 128 - CODE_BASE
    row = lax.broadcasted_iota(jnp.int32, (half, half), 0)
    col = lax.broadcasted_iota(jnp.int32, (half, half), 1)
    ahead = col > row
    low = code[:half]
    high = -1 - code[half:].astype(jnp.float32).T.astype(jnp.int32)
    code = jnp.concatenate([jnp.where(ahead, low, high), jnp.where(ahead, high, low)], axis=1)
    target = jnp.where(code >= 0, code, -1 - code)
    row = lax.broadcasted_iota(jnp.int32, (half, inputs), 0)
    col = lax.broadcasted_iota(jnp.int32, (half, inputs), 1)
    upper = target >= HALF_STACKS
    used = col != row
    goal_ref[...] = jnp.where(upper, target - HALF_STACKS, target).astype(jnp.float32)
    left = jnp.where(used & ~upper, 1.0, 0.0)
    right = jnp.where(used & upper, 1.0, 0.0)
    sign = jnp.where(code >= 0, 1.0, -1.0)
    for n, mask in enumerate((left, right, left * sign, right * sign)):
        mask_ref[n] = mask

    lane = lax.broadcasted_iota(jnp.int32, (half // 2, 128), 1)
    twin[...] = jnp.zeros(twin.shape, jnp.bfloat16)
    for b in range(blocks):
        other[b * 256 : (b + 1) * 256, :] = data_ref[:, b * 256 : (b + 1) * 256].T
        for m in range(2):
            tile = b * 2 + m
            wide[tile * inputs : (tile + 1) * inputs, :] = data_ref[
                :, tile * 128 : (tile + 1) * 128
            ].astype(jnp.float32)
            even = wide[pl.ds(tile * inputs + half, half // 2, stride=2), :]
            odd = wide[pl.ds(tile * inputs + half + 1, half // 2, stride=2), :]
            for part in range(2):
                if part == 0:
                    both = jnp.where(lane < 64, even, pltpu.roll(odd, 64, 1))
                else:
                    both = jnp.where(lane < 64, pltpu.roll(even, 64, 1), odd)
                at = (tile * 2 + part) * (half // 2)
                pairs[at : at + half // 2, :] = both
                source = slice(tile * 128 + part * 64, tile * 128 + part * 64 + 64)
                for side in range(2):
                    at = (b * 2 + part) * 256 + m * 128 + side * 64
                    twin[at : at + 64, side * half : (side + 1) * half] = other[source, half:]
    acc[...] = jnp.zeros(acc.shape, jnp.float32)
    tally[...] = jnp.zeros(tally.shape, jnp.float32)

    def diagonal(rows):
        row = lax.broadcasted_iota(jnp.int32, (rows, 128), 0)
        lane = lax.broadcasted_iota(jnp.int32, (rows, 128), 1)
        channel = jnp.bitwise_and(lane, 15)
        if rows == 32:
            channel = channel + jnp.where(lane >= 64, 16, 0)
        return jnp.where(row == channel, 1.0, 0.0)

    diagonal_32, diagonal_16 = diagonal(32), diagonal(16)
    stack = lax.broadcasted_iota(jnp.int32, (HALF_STACKS, inputs), 0)
    stack = stack.astype(jnp.float32).astype(jnp.bfloat16)

    def spread(reals, imags, mask):
        parts = []
        for u in range(reals.shape[0]):
            real = mask * reals[u : u + 1]
            imag = mask * imags[u : u + 1]
            parts.append(jnp.concatenate([real, imag], axis=1))
            parts.append(jnp.concatenate([imag, -real], axis=1))
        return jnp.concatenate(parts, axis=0).astype(jnp.bfloat16)

    def at_step(g, rows):
        return g * rows if isinstance(g, int) else pl.multiple_of(g * rows, rows)

    def multiply(g):
        start = at_step(g, GROUP)
        start_pair = at_step(g, GROUP // 2)
        row = lax.broadcasted_iota(jnp.int32, (GROUP, half), 0) + start
        col = lax.broadcasted_iota(jnp.int32, (GROUP, half), 1)
        ahead = jnp.where(col > row, 1.0, 0.0)
        for b in range(blocks):
            rows = [wide[pl.ds((b * 2 + m) * inputs + start, GROUP), :] for m in range(2)]
            product = jnp.dot(
                spread(rows[0], rows[1], diagonal_32),
                other[b * 256 : (b + 1) * 256, :],
                preferred_element_type=jnp.float32,
            )
            lower = []
            for part in range(2):
                rows = [
                    pairs[
                        pl.ds(((b * 2 + m) * 2 + part) * (half // 2) + start_pair, GROUP // 2), :
                    ]
                    for m in range(2)
                ]
                at = (b * 2 + part) * 256
                lower.append(
                    jnp.dot(
                        spread(rows[0], rows[1], diagonal_16),
                        twin[at : at + 256, :],
                        preferred_element_type=jnp.float32,
                    )
                )
            for u in range(GROUP):
                side = slice((u % 2) * half, (u % 2 + 1) * half)
                use = jnp.broadcast_to(ahead[u : u + 1], (32, half)) > 0.5
                for p in range(2):
                    mine = product[u * 64 + p * 32 : u * 64 + p * 32 + 32]
                    at = (u // 2) * 32 + p * 16
                    low = jnp.concatenate([x[at : at + 16, side] for x in lower], axis=0)
                    chosen = jnp.where(use, mine[:, :half], low)
                    both = jnp.concatenate([chosen, mine[:, half:]], axis=1)
                    at = (p * blocks + b) * 32
                    held[at : at + 32, u * inputs : (u + 1) * inputs] = both.astype(jnp.bfloat16)

    def accumulate(g):
        start = at_step(g, GROUP)
        goal = goal_ref[pl.ds(start, GROUP), :].astype(jnp.bfloat16)
        masks = [mask_ref[n, pl.ds(start, GROUP), :].astype(jnp.bfloat16) for n in range(4)]
        members, values = [], []
        lefts = rights = None
        for u in range(GROUP):
            columns = slice(u * inputs, (u + 1) * inputs)
            left, right, left_sign, right_sign = [mask[u : u + 1] for mask in masks]
            real = held[: width // 2, columns]
            imag = held[width // 2 :, columns]
            values.append(
                jnp.concatenate(
                    [real * left, imag * left_sign, real * right, imag * right_sign], axis=0
                )
            )
            member = jnp.where(
                stack == goal[u : u + 1], jnp.ones_like(stack), jnp.zeros_like(stack)
            )
            members.append(member)
            lefts = member * left if lefts is None else lefts + member * left
            rights = member * right if rights is None else rights + member * right
        for n, part in enumerate(PARTS):
            acc[n] += lax.dot_general(
                jnp.concatenate(members[part], axis=1),
                jnp.concatenate(values[part], axis=1),
                (((1,), (1,)), ((), ())),
                preferred_element_type=jnp.float32,
            )
        tally[0] += lefts.astype(jnp.float32)
        tally[1] += rights.astype(jnp.float32)

    def step(g, carry):
        accumulate(g)
        multiply(g + 1)
        return carry

    multiply(0)
    lax.fori_loop(0, steps - 1, step, 0)
    accumulate(steps - 1)

    means = []
    for n in range(2):
        counts = jnp.maximum(jnp.sum(tally[n], axis=1, keepdims=True), 1.0)
        total = sum(acc[k, :, n * width : (n + 1) * width] for k in range(len(PARTS)))
        means.append((total / counts).astype(jnp.bfloat16))
    means = jnp.concatenate(means, axis=0)
    moved = jnp.dot(place_ref[...], means, preferred_element_type=jnp.float32)
    out_ref[...] = moved.astype(jnp.bfloat16)


def stack_means(data, place):
    inputs = data.shape[0]
    half = inputs // 2
    lanes = data.shape[1] - half
    width = lanes // SPECTRA
    return pl.pallas_call(
        stack_kernel,
        out_shape=jax.ShapeDtypeStruct((place.shape[0], width), jnp.bfloat16),
        scratch_shapes=[
            pltpu.VMEM((lanes // 128 * inputs, 128), jnp.float32),
            pltpu.VMEM((lanes // 128 * half, 128), jnp.float32),
            pltpu.VMEM((lanes, inputs), jnp.bfloat16),
            pltpu.VMEM((2 * lanes, inputs), jnp.bfloat16),
            pltpu.VMEM((half, inputs), jnp.float32),
            pltpu.VMEM((4, half, inputs), jnp.float32),
            pltpu.VMEM((width, GROUP * inputs), jnp.bfloat16),
            pltpu.VMEM((len(PARTS), HALF_STACKS, 2 * width), jnp.float32),
            pltpu.VMEM((2, HALF_STACKS, inputs), jnp.float32),
        ],
        compiler_params=pltpu.CompilerParams(vmem_limit_bytes=48 * MB),
        name="stack_means",
    )(data, place)


def lay_out_kernel(feeds, padded, capacity, landed_ref, out_ref):
    lane = lax.broadcasted_iota(jnp.int32, (padded, 128), 1)
    for pair in range(feeds // 2):
        left = landed_ref[2 * pair * padded : (2 * pair + 1) * padded, :].astype(jnp.float32)
        right = landed_ref[(2 * pair + 1) * padded : (2 * pair + 2) * padded, :].astype(
            jnp.float32
        )
        real = jnp.where(lane < 64, left, pltpu.roll(right, 64, 1))
        imag = jnp.where(lane < 64, pltpu.roll(left, 64, 1), right)
        for part, value in enumerate((real, imag)):
            out_ref[pl.ds(pair * 2 + part, capacity, stride=feeds), :] = value[:capacity]


def lay_out(landed, feeds, padded, capacity):
    return pl.pallas_call(
        functools.partial(lay_out_kernel, feeds, padded, capacity),
        out_shape=jax.ShapeDtypeStruct((capacity * feeds, 128), jnp.float32),
        compiler_params=pltpu.CompilerParams(vmem_limit_bytes=32 * MB),
        name="lay_out",
    )(landed)


def per_device(raw_samples, stack_code, stack_owner):
    feeds, chans = lax.axis_size("feed"), lax.axis_size("chan")
    devices = feeds * chans
    inputs = raw_samples.shape[0]
    half = stack_code.shape[1] // 2
    everyone = ("feed", "chan")
    share = CHANS // devices
    capacity = 2 * STACKS // feeds
    padded = -(-capacity // 16) * 16
    direct = share == FA and inputs == 8

    owner = jnp.pad(
        stack_owner.astype(jnp.float32), (0, STACK_ROWS - STACKS), constant_values=-1.0
    ).reshape(1, STACK_ROWS)
    place = place_stacks(owner, padded, feeds)

    if direct:
        order = [c * feeds + f for f in range(feeds) for c in range(chans)]
        local = channelize(raw_samples, stack_code, order, True)
        local = local.reshape(devices, inputs, -1)
    else:
        samples = jnp.pad(raw_samples, ((0, -inputs % 8), (0, 0)))
        codes = lax.dynamic_slice_in_dim(stack_code, lax.axis_index("chan") * inputs, inputs)
        codes = jnp.pad(codes, ((0, -inputs % 8), (0, 0)))
        local = channelize(samples, codes, list(range(QS)), False)
        local = local.reshape(QS, samples.shape[0], -1)[:, :inputs]
        codes = jnp.broadcast_to(local[:1, :, 512:], (devices, inputs, half))
        local = local[:, :, :512].reshape(QS, inputs, 2, 2, 2, SPECTRA, 16)
        local = local.transpose(0, 2, 4, 6, 1, 3, 5)
        local = local.reshape(chans, feeds, share // 16, 16, inputs, 2, SPECTRA)
        local = local.transpose(1, 0, 4, 5, 2, 6, 3).reshape(devices, inputs, 8 * share)
        local = jnp.concatenate([local, codes], axis=2)
    moved = lax.all_to_all(local, everyone, split_axis=0, concat_axis=0, tiled=True)
    if not direct:
        codes = moved[:, :, 8 * share :]
        moved = moved[:, :, : 8 * share].reshape(devices, inputs, 2, 4 * share)
        moved = jnp.pad(moved, ((0, 0), (0, 0), (0, 0), (0, 128 - 4 * share)))
        moved = jnp.concatenate([moved.reshape(devices, inputs, 256), codes], axis=2)
    moved = moved.reshape(devices * inputs, -1)

    means = stack_means(moved, place)
    means = means.reshape(feeds, padded, -1)
    landed = lax.all_to_all(means, "feed", split_axis=0, concat_axis=0, tiled=True)
    if direct:
        landed = lay_out(landed.reshape(feeds * padded, -1), feeds, padded, capacity)
        landed = landed.reshape(capacity, feeds // 2, 2, 128).transpose(0, 2, 1, 3)
        return landed.reshape(capacity, 2, feeds * share)
    landed = landed[:, :capacity].reshape(feeds, capacity, 2, -1)[..., :share]
    return landed.transpose(1, 2, 0, 3).reshape(capacity, 2, feeds * share).astype(jnp.float32)


def solution(mesh):
    placed = (P(("feed", "chan"), None), P("feed", None), P())
    return jax.shard_map(
        per_device, mesh=mesh, in_specs=placed, out_specs=P("feed", None, "chan"), check_vma=False
    )
```

```python
import functools
import math

import jax
import jax.numpy as jnp
import numpy as np
from jax import lax
from jax.experimental import pallas as pl
from jax.experimental.pallas import tpu as pltpu
from jax.sharding import PartitionSpec as P

SPECTRA = 4
TAPS = 8
FA = 64
FB = 128
FRAME = 8192
CHANS = 2048
STACKS = 382
QS = CHANS // FA
STACK_ROWS = 384
HALF_STACKS = 192
GROUP = 16
PIECES = 2
CODE_BASE = 384
MB = 1024 * 1024


def window_table():
    length = TAPS * FRAME
    sample = np.arange(length, dtype=np.float64)
    centred = (sample - length / 2 + 0.5) / FRAME
    hanning = 0.5 - 0.5 * np.cos(2.0 * np.pi * (sample + 0.5) / length)
    weights = np.sinc(centred) * hanning
    weights = weights * np.sqrt(FRAME / np.sum(weights * weights))
    return weights.reshape(TAPS, FRAME).astype(np.float32)


def angle_of(left_count, right_count, modulus):
    product = np.arange(left_count)[:, None] * np.arange(right_count)[None, :] % modulus
    return 2.0 * np.pi * product / modulus


def first_table():
    angles = angle_of(FA, FA, FA)
    return np.concatenate([np.cos(angles), -np.sin(angles)], axis=0)


def twiddles():
    angles = angle_of(FA, FB, FRAME)
    return np.cos(angles).astype(np.float32), np.sin(angles).astype(np.float32)


def second_table(order):
    angles = angle_of(FB, QS, FB).T[np.asarray(order)]
    cosine, sine = np.cos(angles), np.sin(angles)
    real_rows = np.concatenate([cosine, sine], axis=1)
    imag_rows = np.concatenate([-sine, cosine], axis=1)
    return np.concatenate([real_rows, imag_rows], axis=0)


def channelize_kernel(
    direct, x_hbm, code_hbm, window_hbm, first_hbm, cos_hbm, sin_hbm, second_hbm, out_ref,
    x_ref, code_ref, window_ref, first_ref, cos_ref, sin_ref, second_ref, frames, mixed, turned,
    x_sems, sems,
):
    inputs = x_ref.shape[0]
    piece = FRAME // PIECES
    pieces = []
    for k in range(PIECES):
        window_copy = pltpu.make_async_copy(
            window_hbm.at[:, k * piece : (k + 1) * piece],
            window_ref.at[:, k * piece : (k + 1) * piece],
            x_sems.at[k, 0],
        )
        window_copy.start()
        copies = [window_copy]
        for r in range(SPECTRA + TAPS - 1):
            at = slice(r * FRAME + k * piece, r * FRAME + (k + 1) * piece)
            copy = pltpu.make_async_copy(x_hbm.at[:, at], x_ref.at[:, at], x_sems.at[k, 1 + r])
            copy.start()
            copies.append(copy)
        pieces.append(copies)
    others = []
    for n, (source, target) in enumerate(
        [
            (code_hbm, code_ref),
            (first_hbm, first_ref),
            (cos_hbm, cos_ref),
            (sin_hbm, sin_ref),
            (second_hbm, second_ref),
        ]
    ):
        copy = pltpu.make_async_copy(source, target, sems.at[n])
        copy.start()
        others.append(copy)

    for a in range(FA):
        if a % (FA // PIECES) == 0:
            for copy in pieces[a // (FA // PIECES)]:
                copy.wait()
        sums = [None] * SPECTRA
        for r in range(SPECTRA + TAPS - 1):
            x = x_ref[:, r * FRAME + a * FB : r * FRAME + (a + 1) * FB].astype(jnp.float32)
            for t in range(SPECTRA):
                if 0 <= r - t < TAPS:
                    term = window_ref[r - t : r - t + 1, a * FB : (a + 1) * FB] * x
                    sums[t] = term if sums[t] is None else sums[t] + term
        for t in range(SPECTRA):
            frames[(t * FA + a) * inputs : (t * FA + a + 1) * inputs, :] = sums[t]
    for copy in others:
        copy.wait()

    count = code_ref.shape[1]
    half = count // 2
    place = lax.axis_index("feed") * lax.axis_size("chan") + lax.axis_index("chan")
    if direct:
        start = pl.multiple_of(lax.axis_index("chan") * inputs, 8)
        codes = code_ref[pl.ds(start, inputs), :]
        first_input = place * inputs
    else:
        codes = code_ref[...]
        first_input = place * (count // (lax.axis_size("feed") * lax.axis_size("chan")))
    row = lax.broadcasted_iota(jnp.int32, (inputs, half), 0) + first_input
    col = lax.broadcasted_iota(jnp.int32, (inputs, half), 1)
    apart = jnp.bitwise_and(col - row, count - 1)
    code = jnp.where((apart >= 1) & (apart <= half), codes[:, :half], codes[:, half:])
    shifted = code + CODE_BASE
    code = jnp.left_shift(128 + jnp.bitwise_and(shifted, 127), jnp.right_shift(shifted, 7))
    code = code.astype(jnp.float32)
    out_ref[:, 512:] = jnp.concatenate([code] * QS, axis=0).astype(jnp.bfloat16)

    for t in range(SPECTRA):
        wide = [frames[pl.ds(t * FA * inputs + i, FA, stride=inputs), :] for i in range(inputs)]
        wide = jnp.concatenate([part.astype(jnp.bfloat16) for part in wide], axis=1)
        section = jnp.dot(first_ref[...], wide, preferred_element_type=jnp.float32)
        for i in range(inputs):
            real = section[:FA, i * FB : (i + 1) * FB]
            imag = section[FA:, i * FB : (i + 1) * FB]
            cosine, sine = cos_ref[...], sin_ref[...]
            twisted = jnp.concatenate(
                [real * cosine + imag * sine, imag * cosine - real * sine], axis=1
            ).astype(jnp.bfloat16)
            for part in range(4):
                start = (i * 4 + part) * 64 + t * 16
                mixed[start : start + 16, :] = twisted[part * 16 : (part + 1) * 16]
    for i in range(inputs):
        spectra = lax.dot_general(
            second_ref[...],
            mixed[i * 256 : (i + 1) * 256, :],
            (((1,), (1,)), ((), ())),
            preferred_element_type=jnp.float32,
        ) * (1.0 / math.sqrt(FRAME))
        for m in range(2):
            for g in range(QS // 8):
                for h in range(2):
                    tile = spectra[m * QS + g * 8 : m * QS + g * 8 + 8, h * 128 : (h + 1) * 128]
                    start = ((h * 2 + m) * QS + g * 8) * inputs + i
                    turned[pl.ds(start, 8, stride=inputs), :] = tile
    for part in range(4):
        rows = turned[part * QS * inputs : (part + 1) * QS * inputs, :]
        out_ref[:, part * 128 : (part + 1) * 128] = rows.astype(jnp.bfloat16)


def channelize(samples, codes, order, direct):
    inputs = samples.shape[0]
    cosine, sine = twiddles()
    operands = (
        samples,
        codes,
        jnp.asarray(window_table()),
        jnp.asarray(first_table(), jnp.bfloat16),
        jnp.asarray(cosine),
        jnp.asarray(sine),
        jnp.asarray(second_table(order), jnp.bfloat16),
    )
    return pl.pallas_call(
        functools.partial(channelize_kernel, direct),
        out_shape=jax.ShapeDtypeStruct((QS * inputs, 512 + codes.shape[1] // 2), jnp.bfloat16),
        in_specs=[pl.BlockSpec(memory_space=pl.ANY)] * len(operands),
        scratch_shapes=[pltpu.VMEM(value.shape, value.dtype) for value in operands]
        + [
            pltpu.VMEM((SPECTRA * inputs * FA, FB), jnp.float32),
            pltpu.VMEM((SPECTRA * inputs * FA, 2 * FB), jnp.bfloat16),
            pltpu.VMEM((4 * QS * inputs, 128), jnp.float32),
            pltpu.SemaphoreType.DMA((PIECES, SPECTRA + TAPS)),
            pltpu.SemaphoreType.DMA((5,)),
        ],
        compiler_params=pltpu.CompilerParams(vmem_limit_bytes=56 * MB),
        name="channelize",
    )(*operands)


def place_kernel(padded, owner_ref, place_ref):
    owner = owner_ref[...]
    across = jnp.broadcast_to(owner, (STACK_ROWS, STACK_ROWS))
    down = across.T
    before = lax.broadcasted_iota(jnp.int32, (STACK_ROWS, STACK_ROWS), 0)
    after = lax.broadcasted_iota(jnp.int32, (STACK_ROWS, STACK_ROWS), 1)
    earlier = jnp.where((across == down) & (before < after), 1.0, 0.0)
    rank = jnp.sum(earlier, axis=0, keepdims=True)
    slot = jnp.where(owner >= 0, owner * padded, -STACK_ROWS) + rank
    slot_id = lax.broadcasted_iota(jnp.int32, place_ref.shape, 0).astype(jnp.float32)
    place_ref[...] = jnp.where(slot_id == slot, 1.0, 0.0).astype(jnp.bfloat16)


def place_stacks(owner, padded, feeds):
    return pl.pallas_call(
        functools.partial(place_kernel, padded),
        out_shape=jax.ShapeDtypeStruct((feeds * padded, STACK_ROWS), jnp.bfloat16),
        compiler_params=pltpu.CompilerParams(vmem_limit_bytes=16 * MB),
        name="place_stacks",
    )(owner)


def stack_kernel(
    data_ref, place_ref, out_ref, wide, pairs, other, twin, goal_ref, mask_ref, held, acc
):
    inputs = data_ref.shape[0]
    half = inputs // 2
    lanes = data_ref.shape[1] - half
    blocks = lanes // 256
    width = lanes // SPECTRA
    steps = half // GROUP

    value = data_ref[:, lanes:].astype(jnp.float32).astype(jnp.int32)
    power = jnp.zeros(value.shape, jnp.int32)
    for e in range(1, 6):
        power = power + jnp.where(value >= 128 << e, 1, 0)
    code = power * 128 + jnp.right_shift(value, power) - 128 - CODE_BASE
    row = lax.broadcasted_iota(jnp.int32, (half, half), 0)
    col = lax.broadcasted_iota(jnp.int32, (half, half), 1)
    ahead = col > row
    low = code[:half]
    high = -1 - code[half:].astype(jnp.float32).T.astype(jnp.int32)
    code = jnp.concatenate([jnp.where(ahead, low, high), jnp.where(ahead, high, low)], axis=1)
    target = jnp.where(code >= 0, code, -1 - code)
    row = lax.broadcasted_iota(jnp.int32, (half, inputs), 0)
    col = lax.broadcasted_iota(jnp.int32, (half, inputs), 1)
    upper = target >= HALF_STACKS
    used = col != row
    goal = jnp.where(upper, target - HALF_STACKS, target).astype(jnp.float32).T
    for g in range(steps):
        rolled = pltpu.roll(goal, (half - g * GROUP) % half, 1) if g else goal
        goal_ref[g * inputs : (g + 1) * inputs, :] = rolled
    left = jnp.where(used & ~upper, 1.0, 0.0)
    right = jnp.where(used & upper, 1.0, 0.0)
    sign = jnp.where(code >= 0, 1.0, -1.0)
    for n, mask in enumerate((left, right, left * sign, right * sign)):
        mask_ref[n] = mask

    lane = lax.broadcasted_iota(jnp.int32, (half // 2, 128), 1)
    twin[...] = jnp.zeros(twin.shape, jnp.bfloat16)
    for b in range(blocks):
        other[b * 256 : (b + 1) * 256, :] = data_ref[:, b * 256 : (b + 1) * 256].T
        for m in range(2):
            tile = b * 2 + m
            wide[tile * inputs : (tile + 1) * inputs, :] = data_ref[
                :, tile * 128 : (tile + 1) * 128
            ].astype(jnp.float32)
            even = wide[pl.ds(tile * inputs + half, half // 2, stride=2), :]
            odd = wide[pl.ds(tile * inputs + half + 1, half // 2, stride=2), :]
            for part in range(2):
                if part == 0:
                    both = jnp.where(lane < 64, even, pltpu.roll(odd, 64, 1))
                else:
                    both = jnp.where(lane < 64, pltpu.roll(even, 64, 1), odd)
                at = (tile * 2 + part) * (half // 2)
                pairs[at : at + half // 2, :] = both
                source = slice(tile * 128 + part * 64, tile * 128 + part * 64 + 64)
                for side in range(2):
                    at = (b * 2 + part) * 256 + m * 128 + side * 64
                    twin[at : at + 64, side * half : (side + 1) * half] = other[source, half:]
    acc[...] = jnp.zeros(acc.shape, jnp.float32)

    def diagonal(rows):
        row = lax.broadcasted_iota(jnp.int32, (rows, 128), 0)
        lane = lax.broadcasted_iota(jnp.int32, (rows, 128), 1)
        channel = jnp.bitwise_and(lane, 15)
        if rows == 32:
            channel = channel + jnp.where(lane >= 64, 16, 0)
        return jnp.where(row == channel, 1.0, 0.0)

    diagonal_32, diagonal_16 = diagonal(32), diagonal(16)
    stack = lax.broadcasted_iota(jnp.int32, (inputs, HALF_STACKS), 1)
    stack = stack.astype(jnp.float32).astype(jnp.bfloat16)
    row = lax.broadcasted_iota(jnp.int32, (16, inputs), 0)
    first_row, second_row = row == 0, row == 1

    def spread(reals, imags, mask):
        parts = []
        for u in range(reals.shape[0]):
            real = mask * reals[u : u + 1]
            imag = mask * imags[u : u + 1]
            parts.append(jnp.concatenate([real, imag], axis=1))
            parts.append(jnp.concatenate([imag, -real], axis=1))
        return jnp.concatenate(parts, axis=0).astype(jnp.bfloat16)

    def multiply(g):
        start, start_pair = g * GROUP, g * GROUP // 2
        row = lax.broadcasted_iota(jnp.int32, (GROUP, half), 0) + start
        col = lax.broadcasted_iota(jnp.int32, (GROUP, half), 1)
        ahead = jnp.where(col > row, 1.0, 0.0)
        for b in range(blocks):
            rows = [wide[pl.ds((b * 2 + m) * inputs + start, GROUP), :] for m in range(2)]
            product = jnp.dot(
                spread(rows[0], rows[1], diagonal_32),
                other[b * 256 : (b + 1) * 256, :],
                preferred_element_type=jnp.float32,
            )
            lower = []
            for part in range(2):
                rows = [
                    pairs[
                        pl.ds(((b * 2 + m) * 2 + part) * (half // 2) + start_pair, GROUP // 2), :
                    ]
                    for m in range(2)
                ]
                at = (b * 2 + part) * 256
                lower.append(
                    jnp.dot(
                        spread(rows[0], rows[1], diagonal_16),
                        twin[at : at + 256, :],
                        preferred_element_type=jnp.float32,
                    )
                )
            for u in range(GROUP):
                side = slice((u % 2) * half, (u % 2 + 1) * half)
                use = jnp.broadcast_to(ahead[u : u + 1], (32, half)) > 0.5
                for p in range(2):
                    mine = product[u * 64 + p * 32 : u * 64 + p * 32 + 32]
                    at = (u // 2) * 32 + p * 16
                    low = jnp.concatenate([x[at : at + 16, side] for x in lower], axis=0)
                    chosen = jnp.where(use, mine[:, :half], low)
                    both = jnp.concatenate([chosen, mine[:, half:]], axis=1)
                    at = (p * blocks + b) * 32
                    held[at : at + 32, u * inputs : (u + 1) * inputs] = both.astype(jnp.bfloat16)

    def accumulate(g):
        start = g * GROUP
        goal = goal_ref[g * inputs : (g + 1) * inputs, :]
        masks = [mask_ref[n, pl.ds(start, GROUP), :].astype(jnp.bfloat16) for n in range(4)]
        members, values = [], []
        for u in range(GROUP):
            columns = slice(u * inputs, (u + 1) * inputs)
            left, right, left_sign, right_sign = [mask[u : u + 1] for mask in masks]
            real = held[: width // 2, columns]
            imag = held[width // 2 :, columns]
            tally = jnp.where(first_row, left, jnp.where(second_row, right, jnp.zeros_like(right)))
            values.append(
                jnp.concatenate(
                    [real * left, imag * left_sign, real * right, imag * right_sign, tally], axis=0
                )
            )
            mine = jnp.broadcast_to(goal[:, u : u + 1], stack.shape).astype(jnp.bfloat16)
            members.append(jnp.where(stack == mine, jnp.ones_like(stack), jnp.zeros_like(stack)))
        acc[...] += jnp.dot(
            jnp.concatenate(values, axis=1),
            jnp.concatenate(members, axis=0),
            preferred_element_type=jnp.float32,
        )

    multiply(0)
    for g in range(steps - 1):
        accumulate(g)
        multiply(g + 1)
    accumulate(steps - 1)

    totals = acc[...].T
    means = []
    for n in range(2):
        counts = jnp.maximum(totals[:, 2 * width + n : 2 * width + n + 1], 1.0)
        total = totals[:, n * width : (n + 1) * width]
        means.append((total / counts).astype(jnp.bfloat16))
    means = jnp.concatenate(means, axis=0)
    moved = jnp.dot(place_ref[...], means, preferred_element_type=jnp.float32)
    out_ref[...] = moved.astype(jnp.bfloat16)


def stack_means(data, place):
    inputs = data.shape[0]
    half = inputs // 2
    lanes = data.shape[1] - half
    width = lanes // SPECTRA
    return pl.pallas_call(
        stack_kernel,
        out_shape=jax.ShapeDtypeStruct((place.shape[0], width), jnp.bfloat16),
        scratch_shapes=[
            pltpu.VMEM((lanes // 128 * inputs, 128), jnp.float32),
            pltpu.VMEM((lanes // 128 * half, 128), jnp.float32),
            pltpu.VMEM((lanes, inputs), jnp.bfloat16),
            pltpu.VMEM((2 * lanes, inputs), jnp.bfloat16),
            pltpu.VMEM((half // GROUP * inputs, half), jnp.float32),
            pltpu.VMEM((4, half, inputs), jnp.float32),
            pltpu.VMEM((width, GROUP * inputs), jnp.bfloat16),
            pltpu.VMEM((2 * width + 16, HALF_STACKS), jnp.float32),
        ],
        compiler_params=pltpu.CompilerParams(vmem_limit_bytes=48 * MB),
        name="stack_means",
    )(data, place)


def lay_out_kernel(feeds, padded, capacity, landed_ref, out_ref):
    lane = lax.broadcasted_iota(jnp.int32, (padded, 128), 1)
    for pair in range(feeds // 2):
        left = landed_ref[2 * pair * padded : (2 * pair + 1) * padded, :].astype(jnp.float32)
        right = landed_ref[(2 * pair + 1) * padded : (2 * pair + 2) * padded, :].astype(
            jnp.float32
        )
        real = jnp.where(lane < 64, left, pltpu.roll(right, 64, 1))
        imag = jnp.where(lane < 64, pltpu.roll(left, 64, 1), right)
        for part, value in enumerate((real, imag)):
            out_ref[pl.ds(pair * 2 + part, capacity, stride=feeds), :] = value[:capacity]


def lay_out(landed, feeds, padded, capacity):
    return pl.pallas_call(
        functools.partial(lay_out_kernel, feeds, padded, capacity),
        out_shape=jax.ShapeDtypeStruct((capacity * feeds, 128), jnp.float32),
        compiler_params=pltpu.CompilerParams(vmem_limit_bytes=32 * MB),
        name="lay_out",
    )(landed)


def per_device(raw_samples, stack_code, stack_owner):
    feeds, chans = lax.axis_size("feed"), lax.axis_size("chan")
    devices = feeds * chans
    inputs = raw_samples.shape[0]
    half = stack_code.shape[1] // 2
    everyone = ("feed", "chan")
    share = CHANS // devices
    capacity = 2 * STACKS // feeds
    padded = -(-capacity // 16) * 16
    direct = share == FA and inputs == 8

    owner = jnp.pad(
        stack_owner.astype(jnp.float32), (0, STACK_ROWS - STACKS), constant_values=-1.0
    ).reshape(1, STACK_ROWS)
    place = place_stacks(owner, padded, feeds)

    if direct:
        order = [c * feeds + f for f in range(feeds) for c in range(chans)]
        local = channelize(raw_samples, stack_code, order, True)
        local = local.reshape(devices, inputs, -1)
    else:
        samples = jnp.pad(raw_samples, ((0, -inputs % 8), (0, 0)))
        codes = lax.dynamic_slice_in_dim(stack_code, lax.axis_index("chan") * inputs, inputs)
        codes = jnp.pad(codes, ((0, -inputs % 8), (0, 0)))
        local = channelize(samples, codes, list(range(QS)), False)
        local = local.reshape(QS, samples.shape[0], -1)[:, :inputs]
        codes = jnp.broadcast_to(local[:1, :, 512:], (devices, inputs, half))
        local = local[:, :, :512].reshape(QS, inputs, 2, 2, 2, SPECTRA, 16)
        local = local.transpose(0, 2, 4, 6, 1, 3, 5)
        local = local.reshape(chans, feeds, share // 16, 16, inputs, 2, SPECTRA)
        local = local.transpose(1, 0, 4, 5, 2, 6, 3).reshape(devices, inputs, 8 * share)
        local = jnp.concatenate([local, codes], axis=2)
    moved = lax.all_to_all(local, everyone, split_axis=0, concat_axis=0, tiled=True)
    if not direct:
        codes = moved[:, :, 8 * share :]
        moved = moved[:, :, : 8 * share].reshape(devices, inputs, 2, 4 * share)
        moved = jnp.pad(moved, ((0, 0), (0, 0), (0, 0), (0, 128 - 4 * share)))
        moved = jnp.concatenate([moved.reshape(devices, inputs, 256), codes], axis=2)
    moved = moved.reshape(devices * inputs, -1)

    means = stack_means(moved, place)
    means = means.reshape(feeds, padded, -1)
    landed = lax.all_to_all(means, "feed", split_axis=0, concat_axis=0, tiled=True)
    if direct:
        landed = lay_out(landed.reshape(feeds * padded, -1), feeds, padded, capacity)
        landed = landed.reshape(capacity, feeds // 2, 2, 128).transpose(0, 2, 1, 3)
        return landed.reshape(capacity, 2, feeds * share)
    landed = landed[:, :capacity].reshape(feeds, capacity, 2, -1)[..., :share]
    return landed.transpose(1, 2, 0, 3).reshape(capacity, 2, feeds * share).astype(jnp.float32)


def solution(mesh):
    placed = (P(("feed", "chan"), None), P("feed", None), P())
    return jax.shard_map(
        per_device, mesh=mesh, in_specs=placed, out_specs=P("feed", None, "chan"), check_vma=False
    )
```

```python
import functools
import math

import jax
import jax.numpy as jnp
import numpy as np
from jax import lax
from jax.experimental import pallas as pl
from jax.experimental.pallas import tpu as pltpu
from jax.sharding import PartitionSpec as P

SPECTRA = 4
TAPS = 8
FA = 64
FB = 128
FRAME = 8192
CHANS = 2048
STACKS = 382
QS = CHANS // FA
STACK_ROWS = 384
HALF_STACKS = 192
GROUP = 32
PIECES = 2
CODE_BASE = 384
MB = 1024 * 1024


def window_table():
    length = TAPS * FRAME
    sample = np.arange(length, dtype=np.float64)
    centred = (sample - length / 2 + 0.5) / FRAME
    hanning = 0.5 - 0.5 * np.cos(2.0 * np.pi * (sample + 0.5) / length)
    weights = np.sinc(centred) * hanning
    weights = weights * np.sqrt(FRAME / np.sum(weights * weights))
    return weights.reshape(TAPS, FRAME).astype(np.float32)


def angle_of(left_count, right_count, modulus):
    product = np.arange(left_count)[:, None] * np.arange(right_count)[None, :] % modulus
    return 2.0 * np.pi * product / modulus


def first_table():
    angles = angle_of(FA, FA, FA)
    return np.concatenate([np.cos(angles), -np.sin(angles)], axis=0)


def twiddles():
    angles = angle_of(FA, FB, FRAME)
    return np.cos(angles).astype(np.float32), np.sin(angles).astype(np.float32)


def second_table(order):
    angles = angle_of(FB, QS, FB).T[np.asarray(order)]
    cosine, sine = np.cos(angles), np.sin(angles)
    real_rows = np.concatenate([cosine, sine], axis=1)
    imag_rows = np.concatenate([-sine, cosine], axis=1)
    return np.concatenate([real_rows, imag_rows], axis=0)


def channelize_kernel(
    direct, x_hbm, code_hbm, window_hbm, first_hbm, cos_hbm, sin_hbm, second_hbm, out_ref,
    x_ref, code_ref, window_ref, first_ref, cos_ref, sin_ref, second_ref, frames, mixed, turned,
    x_sems, sems,
):
    inputs = x_ref.shape[0]
    piece = FRAME // PIECES
    pieces = []
    for k in range(PIECES):
        window_copy = pltpu.make_async_copy(
            window_hbm.at[:, k * piece : (k + 1) * piece],
            window_ref.at[:, k * piece : (k + 1) * piece],
            x_sems.at[k, 0],
        )
        window_copy.start()
        copies = [window_copy]
        for r in range(SPECTRA + TAPS - 1):
            at = slice(r * FRAME + k * piece, r * FRAME + (k + 1) * piece)
            copy = pltpu.make_async_copy(x_hbm.at[:, at], x_ref.at[:, at], x_sems.at[k, 1 + r])
            copy.start()
            copies.append(copy)
        pieces.append(copies)
    others = []
    for n, (source, target) in enumerate(
        [
            (code_hbm, code_ref),
            (first_hbm, first_ref),
            (cos_hbm, cos_ref),
            (sin_hbm, sin_ref),
            (second_hbm, second_ref),
        ]
    ):
        copy = pltpu.make_async_copy(source, target, sems.at[n])
        copy.start()
        others.append(copy)

    for a in range(FA):
        if a % (FA // PIECES) == 0:
            for copy in pieces[a // (FA // PIECES)]:
                copy.wait()
        sums = [None] * SPECTRA
        for r in range(SPECTRA + TAPS - 1):
            x = x_ref[:, r * FRAME + a * FB : r * FRAME + (a + 1) * FB].astype(jnp.float32)
            for t in range(SPECTRA):
                if 0 <= r - t < TAPS:
                    term = window_ref[r - t : r - t + 1, a * FB : (a + 1) * FB] * x
                    sums[t] = term if sums[t] is None else sums[t] + term
        for t in range(SPECTRA):
            frames[(t * FA + a) * inputs : (t * FA + a + 1) * inputs, :] = sums[t]
    for copy in others:
        copy.wait()

    count = code_ref.shape[1]
    half = count // 2
    place = lax.axis_index("feed") * lax.axis_size("chan") + lax.axis_index("chan")
    if direct:
        start = pl.multiple_of(lax.axis_index("chan") * inputs, 8)
        codes = code_ref[pl.ds(start, inputs), :]
        first_input = place * inputs
    else:
        codes = code_ref[...]
        first_input = place * (count // (lax.axis_size("feed") * lax.axis_size("chan")))
    row = lax.broadcasted_iota(jnp.int32, (inputs, half), 0) + first_input
    col = lax.broadcasted_iota(jnp.int32, (inputs, half), 1)
    apart = jnp.bitwise_and(col - row, count - 1)
    code = jnp.where((apart >= 1) & (apart <= half), codes[:, :half], codes[:, half:])
    shifted = code + CODE_BASE
    code = jnp.left_shift(128 + jnp.bitwise_and(shifted, 127), jnp.right_shift(shifted, 7))
    code = code.astype(jnp.float32)
    out_ref[:, 512:] = jnp.concatenate([code] * QS, axis=0).astype(jnp.bfloat16)

    for t in range(SPECTRA):
        wide = [frames[pl.ds(t * FA * inputs + i, FA, stride=inputs), :] for i in range(inputs)]
        wide = jnp.concatenate([part.astype(jnp.bfloat16) for part in wide], axis=1)
        section = jnp.dot(first_ref[...], wide, preferred_element_type=jnp.float32)
        for i in range(inputs):
            real = section[:FA, i * FB : (i + 1) * FB]
            imag = section[FA:, i * FB : (i + 1) * FB]
            cosine, sine = cos_ref[...], sin_ref[...]
            twisted = jnp.concatenate(
                [real * cosine + imag * sine, imag * cosine - real * sine], axis=1
            ).astype(jnp.bfloat16)
            for part in range(4):
                start = (i * 4 + part) * 64 + t * 16
                mixed[start : start + 16, :] = twisted[part * 16 : (part + 1) * 16]
    for i in range(inputs):
        spectra = lax.dot_general(
            second_ref[...],
            mixed[i * 256 : (i + 1) * 256, :],
            (((1,), (1,)), ((), ())),
            preferred_element_type=jnp.float32,
        ) * (1.0 / math.sqrt(FRAME))
        for m in range(2):
            for g in range(QS // 8):
                for h in range(2):
                    tile = spectra[m * QS + g * 8 : m * QS + g * 8 + 8, h * 128 : (h + 1) * 128]
                    start = ((h * 2 + m) * QS + g * 8) * inputs + i
                    turned[pl.ds(start, 8, stride=inputs), :] = tile
    for part in range(4):
        rows = turned[part * QS * inputs : (part + 1) * QS * inputs, :]
        out_ref[:, part * 128 : (part + 1) * 128] = rows.astype(jnp.bfloat16)


def channelize(samples, codes, order, direct):
    inputs = samples.shape[0]
    cosine, sine = twiddles()
    operands = (
        samples,
        codes,
        jnp.asarray(window_table()),
        jnp.asarray(first_table(), jnp.bfloat16),
        jnp.asarray(cosine),
        jnp.asarray(sine),
        jnp.asarray(second_table(order), jnp.bfloat16),
    )
    return pl.pallas_call(
        functools.partial(channelize_kernel, direct),
        out_shape=jax.ShapeDtypeStruct((QS * inputs, 512 + codes.shape[1] // 2), jnp.bfloat16),
        in_specs=[pl.BlockSpec(memory_space=pl.ANY)] * len(operands),
        scratch_shapes=[pltpu.VMEM(value.shape, value.dtype) for value in operands]
        + [
            pltpu.VMEM((SPECTRA * inputs * FA, FB), jnp.float32),
            pltpu.VMEM((SPECTRA * inputs * FA, 2 * FB), jnp.bfloat16),
            pltpu.VMEM((4 * QS * inputs, 128), jnp.float32),
            pltpu.SemaphoreType.DMA((PIECES, SPECTRA + TAPS)),
            pltpu.SemaphoreType.DMA((5,)),
        ],
        compiler_params=pltpu.CompilerParams(vmem_limit_bytes=56 * MB),
        name="channelize",
    )(*operands)


def place_kernel(padded, owner_ref, place_ref):
    owner = owner_ref[...]
    across = jnp.broadcast_to(owner, (STACK_ROWS, STACK_ROWS))
    down = across.T
    before = lax.broadcasted_iota(jnp.int32, (STACK_ROWS, STACK_ROWS), 0)
    after = lax.broadcasted_iota(jnp.int32, (STACK_ROWS, STACK_ROWS), 1)
    earlier = jnp.where((across == down) & (before < after), 1.0, 0.0)
    rank = jnp.sum(earlier, axis=0, keepdims=True)
    slot = jnp.where(owner >= 0, owner * padded, -STACK_ROWS) + rank
    slot_id = lax.broadcasted_iota(jnp.int32, (place_ref.shape[0], STACK_ROWS), 0)
    place = jnp.where(slot_id.astype(jnp.float32) == slot, 1.0, 0.0)
    place_ref[...] = jnp.zeros(place_ref.shape, jnp.bfloat16)
    for n in range(2):
        half = place[:, n * HALF_STACKS : (n + 1) * HALF_STACKS].astype(jnp.bfloat16)
        place_ref[:, n * 256 : n * 256 + HALF_STACKS] = half


def place_stacks(owner, padded, feeds):
    return pl.pallas_call(
        functools.partial(place_kernel, padded),
        out_shape=jax.ShapeDtypeStruct((feeds * padded, 512), jnp.bfloat16),
        compiler_params=pltpu.CompilerParams(vmem_limit_bytes=16 * MB),
        name="place_stacks",
    )(owner)


def decode(codes):
    inputs = codes.shape[0]
    half = inputs // 2
    value = codes.astype(jnp.float32).astype(jnp.int32)
    power = jnp.zeros(value.shape, jnp.int32)
    for e in range(1, 6):
        power = power + jnp.where(value >= 128 << e, 1, 0)
    code = power * 128 + jnp.right_shift(value, power) - 128 - CODE_BASE
    row = lax.broadcasted_iota(jnp.int32, (half, half), 0)
    col = lax.broadcasted_iota(jnp.int32, (half, half), 1)
    ahead = col > row
    low = code[:half]
    high = -1 - code[half:].astype(jnp.float32).T.astype(jnp.int32)
    code = jnp.concatenate([jnp.where(ahead, low, high), jnp.where(ahead, high, low)], axis=1)
    target = jnp.where(code >= 0, code, -1 - code)
    row = lax.broadcasted_iota(jnp.int32, (half, inputs), 0)
    col = lax.broadcasted_iota(jnp.int32, (half, inputs), 1)
    return target, col != row, jnp.where(code >= 0, 1.0, -1.0)


def stack_kernel(
    data_ref, place_ref, out_ref, wide, pairs, other, twin, goal_ref, mask_ref, held, acc
):
    inputs = data_ref.shape[0]
    half = inputs // 2
    lanes = data_ref.shape[1] - half
    blocks = lanes // 256
    width = lanes // SPECTRA
    steps = half // GROUP

    target, used, sign = decode(data_ref[:, lanes:])
    upper = target >= HALF_STACKS
    goal = jnp.where(upper, target - HALF_STACKS, target).astype(jnp.float32).T
    for g in range(steps):
        rolled = pltpu.roll(goal, (half - g * GROUP) % half, 1) if g else goal
        goal_ref[g * inputs : (g + 1) * inputs, :] = rolled
    left = jnp.where(used & ~upper, 1.0, 0.0)
    right = jnp.where(used & upper, 1.0, 0.0)
    for n, mask in enumerate((left, right, left * sign, right * sign)):
        mask_ref[n] = mask

    lane = lax.broadcasted_iota(jnp.int32, (half // 2, 128), 1)
    twin[...] = jnp.zeros(twin.shape, jnp.bfloat16)
    for b in range(blocks):
        other[b * 256 : (b + 1) * 256, :] = data_ref[:, b * 256 : (b + 1) * 256].T
        for m in range(2):
            tile = b * 2 + m
            wide[tile * inputs : (tile + 1) * inputs, :] = data_ref[
                :, tile * 128 : (tile + 1) * 128
            ].astype(jnp.float32)
            even = wide[pl.ds(tile * inputs + half, half // 2, stride=2), :]
            odd = wide[pl.ds(tile * inputs + half + 1, half // 2, stride=2), :]
            for part in range(2):
                if part == 0:
                    both = jnp.where(lane < 64, even, pltpu.roll(odd, 64, 1))
                else:
                    both = jnp.where(lane < 64, pltpu.roll(even, 64, 1), odd)
                at = (tile * 2 + part) * (half // 2)
                pairs[at : at + half // 2, :] = both
                source = slice(tile * 128 + part * 64, tile * 128 + part * 64 + 64)
                for side in range(2):
                    at = (b * 2 + part) * 256 + m * 128 + side * 64
                    twin[at : at + 64, side * half : (side + 1) * half] = other[source, half:]
    acc[...] = jnp.zeros(acc.shape, jnp.float32)

    def diagonal(rows):
        row = lax.broadcasted_iota(jnp.int32, (rows, 128), 0)
        lane = lax.broadcasted_iota(jnp.int32, (rows, 128), 1)
        channel = jnp.bitwise_and(lane, 15)
        if rows == 32:
            channel = channel + jnp.where(lane >= 64, 16, 0)
        return jnp.where(row == channel, 1.0, 0.0)

    diagonal_32, diagonal_16 = diagonal(32), diagonal(16)
    stack = lax.broadcasted_iota(jnp.int32, (inputs, HALF_STACKS), 1)
    stack = stack.astype(jnp.float32).astype(jnp.bfloat16)
    row = lax.broadcasted_iota(jnp.int32, (16, inputs), 0)
    first_row, second_row = row == 0, row == 1

    def spread(reals, imags, mask):
        parts = []
        for u in range(reals.shape[0]):
            real = mask * reals[u : u + 1]
            imag = mask * imags[u : u + 1]
            parts.append(jnp.concatenate([real, imag], axis=1))
            parts.append(jnp.concatenate([imag, -real], axis=1))
        return jnp.concatenate(parts, axis=0).astype(jnp.bfloat16)

    def multiply(g):
        start, start_pair = g * GROUP, g * GROUP // 2
        row = lax.broadcasted_iota(jnp.int32, (GROUP, half), 0) + start
        col = lax.broadcasted_iota(jnp.int32, (GROUP, half), 1)
        ahead = jnp.where(col > row, 1.0, 0.0)
        for b in range(blocks):
            rows = [wide[pl.ds((b * 2 + m) * inputs + start, GROUP), :] for m in range(2)]
            product = jnp.dot(
                spread(rows[0], rows[1], diagonal_32),
                other[b * 256 : (b + 1) * 256, :],
                preferred_element_type=jnp.float32,
            )
            lower = []
            for part in range(2):
                rows = [
                    pairs[
                        pl.ds(((b * 2 + m) * 2 + part) * (half // 2) + start_pair, GROUP // 2), :
                    ]
                    for m in range(2)
                ]
                at = (b * 2 + part) * 256
                lower.append(
                    jnp.dot(
                        spread(rows[0], rows[1], diagonal_16),
                        twin[at : at + 256, :],
                        preferred_element_type=jnp.float32,
                    )
                )
            for u in range(GROUP):
                side = slice((u % 2) * half, (u % 2 + 1) * half)
                use = jnp.broadcast_to(ahead[u : u + 1], (32, half)) > 0.5
                for p in range(2):
                    mine = product[u * 64 + p * 32 : u * 64 + p * 32 + 32]
                    at = (u // 2) * 32 + p * 16
                    low = jnp.concatenate([x[at : at + 16, side] for x in lower], axis=0)
                    chosen = jnp.where(use, mine[:, :half], low)
                    both = jnp.concatenate([chosen, mine[:, half:]], axis=1)
                    at = (p * blocks + b) * 32
                    held[at : at + 32, u * inputs : (u + 1) * inputs] = both.astype(jnp.bfloat16)

    def accumulate(g):
        start = g * GROUP
        goal = goal_ref[g * inputs : (g + 1) * inputs, :]
        masks = [mask_ref[n, pl.ds(start, GROUP), :].astype(jnp.bfloat16) for n in range(4)]
        members, values = [], []
        for u in range(GROUP):
            columns = slice(u * inputs, (u + 1) * inputs)
            left, right, left_sign, right_sign = [mask[u : u + 1] for mask in masks]
            real = held[: width // 2, columns]
            imag = held[width // 2 :, columns]
            tally = jnp.where(first_row, left, jnp.where(second_row, right, jnp.zeros_like(right)))
            values.append(
                jnp.concatenate(
                    [real * left, imag * left_sign, real * right, imag * right_sign, tally], axis=0
                )
            )
            mine = jnp.broadcast_to(goal[:, u : u + 1], stack.shape).astype(jnp.bfloat16)
            members.append(jnp.where(stack == mine, jnp.ones_like(stack), jnp.zeros_like(stack)))
        acc[...] += jnp.dot(
            jnp.concatenate(values, axis=1),
            jnp.concatenate(members, axis=0),
            preferred_element_type=jnp.float32,
        )

    multiply(0)
    for g in range(steps - 1):
        accumulate(g)
        multiply(g + 1)
    accumulate(steps - 1)

    means = []
    for n in range(2):
        counts = jnp.maximum(acc[2 * width + n : 2 * width + n + 1, :], 1.0)
        means.append((acc[n * width : (n + 1) * width, :] / counts).astype(jnp.bfloat16))
    moved = [
        lax.dot_general(
            place_ref[:, n * 256 : n * 256 + HALF_STACKS],
            means[n],
            (((1,), (1,)), ((), ())),
            preferred_element_type=jnp.float32,
        )
        for n in range(2)
    ]
    out_ref[...] = (moved[0] + moved[1]).astype(jnp.bfloat16)


def stack_means(data, place):
    inputs = data.shape[0]
    half = inputs // 2
    lanes = data.shape[1] - half
    width = lanes // SPECTRA
    return pl.pallas_call(
        stack_kernel,
        out_shape=jax.ShapeDtypeStruct((place.shape[0], width), jnp.bfloat16),
        scratch_shapes=[
            pltpu.VMEM((lanes // 128 * inputs, 128), jnp.float32),
            pltpu.VMEM((lanes // 128 * half, 128), jnp.float32),
            pltpu.VMEM((lanes, inputs), jnp.bfloat16),
            pltpu.VMEM((2 * lanes, inputs), jnp.bfloat16),
            pltpu.VMEM((half // GROUP * inputs, half), jnp.float32),
            pltpu.VMEM((4, half, inputs), jnp.float32),
            pltpu.VMEM((width, GROUP * inputs), jnp.bfloat16),
            pltpu.VMEM((2 * width + 16, HALF_STACKS), jnp.float32),
        ],
        compiler_params=pltpu.CompilerParams(vmem_limit_bytes=48 * MB),
        name="stack_means",
    )(data, place)


def lay_out_kernel(feeds, padded, capacity, landed_ref, out_ref):
    lane = lax.broadcasted_iota(jnp.int32, (padded, 128), 1)
    for pair in range(feeds // 2):
        left = landed_ref[2 * pair * padded : (2 * pair + 1) * padded, :].astype(jnp.float32)
        right = landed_ref[(2 * pair + 1) * padded : (2 * pair + 2) * padded, :].astype(
            jnp.float32
        )
        real = jnp.where(lane < 64, left, pltpu.roll(right, 64, 1))
        imag = jnp.where(lane < 64, pltpu.roll(left, 64, 1), right)
        for part, value in enumerate((real, imag)):
            out_ref[pl.ds(pair * 2 + part, capacity, stride=feeds), :] = value[:capacity]


def lay_out(landed, feeds, padded, capacity):
    return pl.pallas_call(
        functools.partial(lay_out_kernel, feeds, padded, capacity),
        out_shape=jax.ShapeDtypeStruct((capacity * feeds, 128), jnp.float32),
        compiler_params=pltpu.CompilerParams(vmem_limit_bytes=32 * MB),
        name="lay_out",
    )(landed)


def per_device(raw_samples, stack_code, stack_owner):
    feeds, chans = lax.axis_size("feed"), lax.axis_size("chan")
    devices = feeds * chans
    inputs = raw_samples.shape[0]
    half = stack_code.shape[1] // 2
    everyone = ("feed", "chan")
    share = CHANS // devices
    capacity = 2 * STACKS // feeds
    padded = -(-capacity // 16) * 16
    direct = share == FA and inputs == 8

    owner = jnp.pad(
        stack_owner.astype(jnp.float32), (0, STACK_ROWS - STACKS), constant_values=-1.0
    ).reshape(1, STACK_ROWS)
    place = place_stacks(owner, padded, feeds)

    if direct:
        order = [c * feeds + f for f in range(feeds) for c in range(chans)]
        local = channelize(raw_samples, stack_code, order, True)
        local = local.reshape(devices, inputs, -1)
    else:
        samples = jnp.pad(raw_samples, ((0, -inputs % 8), (0, 0)))
        codes = lax.dynamic_slice_in_dim(stack_code, lax.axis_index("chan") * inputs, inputs)
        codes = jnp.pad(codes, ((0, -inputs % 8), (0, 0)))
        local = channelize(samples, codes, list(range(QS)), False)
        local = local.reshape(QS, samples.shape[0], -1)[:, :inputs]
        codes = jnp.broadcast_to(local[:1, :, 512:], (devices, inputs, half))
        local = local[:, :, :512].reshape(QS, inputs, 2, 2, 2, SPECTRA, 16)
        local = local.transpose(0, 2, 4, 6, 1, 3, 5)
        local = local.reshape(chans, feeds, share // 16, 16, inputs, 2, SPECTRA)
        local = local.transpose(1, 0, 4, 5, 2, 6, 3).reshape(devices, inputs, 8 * share)
        local = jnp.concatenate([local, codes], axis=2)
    moved = lax.all_to_all(local, everyone, split_axis=0, concat_axis=0, tiled=True)
    if not direct:
        codes = moved[:, :, 8 * share :]
        moved = moved[:, :, : 8 * share].reshape(devices, inputs, 2, 4 * share)
        moved = jnp.pad(moved, ((0, 0), (0, 0), (0, 0), (0, 128 - 4 * share)))
        moved = jnp.concatenate([moved.reshape(devices, inputs, 256), codes], axis=2)
    moved = moved.reshape(devices * inputs, -1)

    means = stack_means(moved, place)
    landed = lax.all_to_all(
        means.reshape(feeds, padded, -1), "feed", split_axis=0, concat_axis=0, tiled=True
    )
    if direct:
        landed = lay_out(landed.reshape(feeds * padded, -1), feeds, padded, capacity)
        landed = landed.reshape(capacity, feeds // 2, 2, 128).transpose(0, 2, 1, 3)
        return landed.reshape(capacity, 2, feeds * share)
    landed = landed[:, :capacity].reshape(feeds, capacity, 2, -1)[..., :share]
    return landed.transpose(1, 2, 0, 3).reshape(capacity, 2, feeds * share).astype(jnp.float32)


def solution(mesh):
    placed = (P(("feed", "chan"), None), P("feed", None), P())
    return jax.shard_map(
        per_device, mesh=mesh, in_specs=placed, out_specs=P("feed", None, "chan"), check_vma=False
    )
```

```python
import functools
import math

import jax
import jax.numpy as jnp
import numpy as np
from jax import lax
from jax.experimental import pallas as pl
from jax.experimental.pallas import tpu as pltpu
from jax.sharding import PartitionSpec as P

SPECTRA = 4
TAPS = 8
FA = 64
FB = 128
FRAME = 8192
CHANS = 2048
STACKS = 382
QS = CHANS // FA
STACK_ROWS = 384
HALF_STACKS = 192
GROUP = 32
PIECES = 2
AHEAD = 2
CODE_BASE = 384
MB = 1024 * 1024


def window_table():
    length = TAPS * FRAME
    sample = np.arange(length, dtype=np.float64)
    centred = (sample - length / 2 + 0.5) / FRAME
    hanning = 0.5 - 0.5 * np.cos(2.0 * np.pi * (sample + 0.5) / length)
    weights = np.sinc(centred) * hanning
    weights = weights * np.sqrt(FRAME / np.sum(weights * weights))
    return weights.reshape(TAPS, FRAME).astype(np.float32)


def angle_of(left_count, right_count, modulus):
    product = np.arange(left_count)[:, None] * np.arange(right_count)[None, :] % modulus
    return 2.0 * np.pi * product / modulus


def first_table():
    angles = angle_of(FA, FA, FA)
    return np.concatenate([np.cos(angles), -np.sin(angles)], axis=0)


def twiddles():
    angles = angle_of(FA, FB, FRAME)
    return np.cos(angles).astype(np.float32), np.sin(angles).astype(np.float32)


def second_table(order):
    angles = angle_of(FB, QS, FB).T[np.asarray(order)]
    cosine, sine = np.cos(angles), np.sin(angles)
    real_rows = np.concatenate([cosine, sine], axis=1)
    imag_rows = np.concatenate([-sine, cosine], axis=1)
    return np.concatenate([real_rows, imag_rows], axis=0)


def channelize_kernel(
    direct, x_hbm, code_hbm, window_hbm, first_hbm, cos_hbm, sin_hbm, second_hbm, out_hbm,
    x_ref, code_ref, window_ref, first_ref, cos_ref, sin_ref, second_ref, frames, mixed, turned,
    out_ref, x_sems, sems, out_sems,
):
    inputs = x_ref.shape[0]
    piece = FRAME // PIECES
    pieces = {}

    def fetch(k):
        at = slice(k * piece, (k + 1) * piece)
        copies = [
            pltpu.make_async_copy(window_hbm.at[:, at], window_ref.at[:, at], x_sems.at[k, 0])
        ]
        for r in range(SPECTRA + TAPS - 1):
            at = slice(r * FRAME + k * piece, r * FRAME + (k + 1) * piece)
            copies.append(
                pltpu.make_async_copy(x_hbm.at[:, at], x_ref.at[:, at], x_sems.at[k, 1 + r])
            )
        for copy in copies:
            copy.start()
        pieces[k] = copies

    for k in range(min(AHEAD, PIECES)):
        fetch(k)
    others = [
        pltpu.make_async_copy(source, target, sems.at[n])
        for n, (source, target) in enumerate(
            [
                (code_hbm, code_ref),
                (first_hbm, first_ref),
                (cos_hbm, cos_ref),
                (sin_hbm, sin_ref),
                (second_hbm, second_ref),
            ]
        )
    ]
    for copy in others:
        copy.start()

    for k in range(PIECES):
        for copy in pieces[k]:
            copy.wait()
        if k + AHEAD < PIECES:
            fetch(k + AHEAD)
        for a in range(k * FA // PIECES, (k + 1) * FA // PIECES):
            sums = [None] * SPECTRA
            for r in range(SPECTRA + TAPS - 1):
                x = x_ref[:, r * FRAME + a * FB : r * FRAME + (a + 1) * FB].astype(jnp.float32)
                for t in range(SPECTRA):
                    if 0 <= r - t < TAPS:
                        term = window_ref[r - t : r - t + 1, a * FB : (a + 1) * FB] * x
                        sums[t] = term if sums[t] is None else sums[t] + term
            for t in range(SPECTRA):
                frames[(t * FA + a) * inputs : (t * FA + a + 1) * inputs, :] = sums[t]
    for copy in others:
        copy.wait()

    count = code_ref.shape[1]
    half = count // 2
    place = lax.axis_index("feed") * lax.axis_size("chan") + lax.axis_index("chan")
    if direct:
        start = pl.multiple_of(lax.axis_index("chan") * inputs, 8)
        codes = code_ref[pl.ds(start, inputs), :]
        first_input = place * inputs
    else:
        codes = code_ref[...]
        first_input = place * (count // (lax.axis_size("feed") * lax.axis_size("chan")))
    row = lax.broadcasted_iota(jnp.int32, (inputs, half), 0) + first_input
    col = lax.broadcasted_iota(jnp.int32, (inputs, half), 1)
    apart = jnp.bitwise_and(col - row, count - 1)
    code = jnp.where((apart >= 1) & (apart <= half), codes[:, :half], codes[:, half:])
    shifted = code + CODE_BASE
    code = jnp.left_shift(128 + jnp.bitwise_and(shifted, 127), jnp.right_shift(shifted, 7))
    code = code.astype(jnp.float32)
    out_ref[:, 512:] = jnp.concatenate([code] * QS, axis=0).astype(jnp.bfloat16)

    def send(n, at):
        copy = pltpu.make_async_copy(out_ref.at[:, at], out_hbm.at[:, at], out_sems.at[n])
        copy.start()
        return copy

    sent = [send(2, slice(512, 512 + half))]

    for t in range(SPECTRA):
        for pair in range(inputs // 2):
            wide = [
                frames[pl.ds(t * FA * inputs + i, FA, stride=inputs), :].astype(jnp.bfloat16)
                for i in (2 * pair, 2 * pair + 1)
            ]
            section = jnp.dot(
                first_ref[...],
                jnp.concatenate(wide, axis=1),
                preferred_element_type=jnp.float32,
            )
            cosine, sine = cos_ref[...], sin_ref[...]
            for i in range(2):
                real = section[:FA, i * FB : (i + 1) * FB]
                imag = section[FA:, i * FB : (i + 1) * FB]
                twisted = jnp.concatenate(
                    [real * cosine + imag * sine, imag * cosine - real * sine], axis=1
                ).astype(jnp.bfloat16)
                for part in range(4):
                    start = (part // 2 * inputs + 2 * pair + i) * 128 + part % 2 * 64 + t * 16
                    mixed[start : start + 16, :] = twisted[part * 16 : (part + 1) * 16]
    for h in range(2):
        for pair in range(inputs // 2):
            start = (h * inputs + 2 * pair) * 128
            spectra = lax.dot_general(
                second_ref[...],
                mixed[start : start + 256, :],
                (((1,), (1,)), ((), ())),
                preferred_element_type=jnp.float32,
            ) * (1.0 / math.sqrt(FRAME))
            for i in range(2):
                for m in range(2):
                    for g in range(QS // 8):
                        row = m * QS + g * 8
                        start = ((h * 2 + m) * QS + g * 8) * inputs + 2 * pair + i
                        turned[pl.ds(start, 8, stride=inputs), :] = spectra[
                            row : row + 8, i * 128 : (i + 1) * 128
                        ]
        for part in (2 * h, 2 * h + 1):
            rows = turned[part * QS * inputs : (part + 1) * QS * inputs, :]
            out_ref[:, part * 128 : (part + 1) * 128] = rows.astype(jnp.bfloat16)
        sent.append(send(h, slice(h * 256, h * 256 + 256)))
    for copy in sent:
        copy.wait()


def channelize(samples, codes, order, direct):
    inputs = samples.shape[0]
    cosine, sine = twiddles()
    operands = (
        samples,
        codes,
        jnp.asarray(window_table()),
        jnp.asarray(first_table(), jnp.bfloat16),
        jnp.asarray(cosine),
        jnp.asarray(sine),
        jnp.asarray(second_table(order), jnp.bfloat16),
    )
    return pl.pallas_call(
        functools.partial(channelize_kernel, direct),
        out_shape=jax.ShapeDtypeStruct((QS * inputs, 512 + codes.shape[1] // 2), jnp.bfloat16),
        in_specs=[pl.BlockSpec(memory_space=pl.ANY)] * len(operands),
        out_specs=pl.BlockSpec(memory_space=pl.ANY),
        scratch_shapes=[pltpu.VMEM(value.shape, value.dtype) for value in operands]
        + [
            pltpu.VMEM((SPECTRA * inputs * FA, FB), jnp.float32),
            pltpu.VMEM((SPECTRA * inputs * FA, 2 * FB), jnp.bfloat16),
            pltpu.VMEM((4 * QS * inputs, 128), jnp.float32),
            pltpu.VMEM((QS * inputs, 512 + codes.shape[1] // 2), jnp.bfloat16),
            pltpu.SemaphoreType.DMA((PIECES, SPECTRA + TAPS)),
            pltpu.SemaphoreType.DMA((5,)),
            pltpu.SemaphoreType.DMA((3,)),
        ],
        compiler_params=pltpu.CompilerParams(vmem_limit_bytes=56 * MB),
        name="channelize",
    )(*operands)


def place_kernel(padded, owner_ref, place_ref):
    owner = owner_ref[...]
    across = jnp.broadcast_to(owner, (STACK_ROWS, STACK_ROWS))
    down = across.T
    before = lax.broadcasted_iota(jnp.int32, (STACK_ROWS, STACK_ROWS), 0)
    after = lax.broadcasted_iota(jnp.int32, (STACK_ROWS, STACK_ROWS), 1)
    earlier = jnp.where((across == down) & (before < after), 1.0, 0.0)
    rank = jnp.sum(earlier, axis=0, keepdims=True)
    slot = jnp.where(owner >= 0, owner * padded, -STACK_ROWS) + rank
    slot_id = lax.broadcasted_iota(jnp.int32, (place_ref.shape[0], STACK_ROWS), 0)
    place = jnp.where(slot_id.astype(jnp.float32) == slot, 1.0, 0.0)
    place_ref[...] = jnp.zeros(place_ref.shape, jnp.bfloat16)
    for n in range(2):
        half = place[:, n * HALF_STACKS : (n + 1) * HALF_STACKS].astype(jnp.bfloat16)
        place_ref[:, n * 256 : n * 256 + HALF_STACKS] = half


def place_stacks(owner, padded, feeds):
    return pl.pallas_call(
        functools.partial(place_kernel, padded),
        out_shape=jax.ShapeDtypeStruct((feeds * padded, 512), jnp.bfloat16),
        compiler_params=pltpu.CompilerParams(vmem_limit_bytes=16 * MB),
        name="place_stacks",
    )(owner)


def decode(codes):
    inputs = codes.shape[0]
    half = inputs // 2
    value = codes.astype(jnp.float32).astype(jnp.int32)
    power = jnp.zeros(value.shape, jnp.int32)
    for e in range(1, 6):
        power = power + jnp.where(value >= 128 << e, 1, 0)
    code = power * 128 + jnp.right_shift(value, power) - 128 - CODE_BASE
    row = lax.broadcasted_iota(jnp.int32, (half, half), 0)
    col = lax.broadcasted_iota(jnp.int32, (half, half), 1)
    ahead = col > row
    low = code[:half]
    high = -1 - code[half:].astype(jnp.float32).T.astype(jnp.int32)
    code = jnp.concatenate([jnp.where(ahead, low, high), jnp.where(ahead, high, low)], axis=1)
    target = jnp.where(code >= 0, code, -1 - code)
    row = lax.broadcasted_iota(jnp.int32, (half, inputs), 0)
    col = lax.broadcasted_iota(jnp.int32, (half, inputs), 1)
    return target, col != row, jnp.where(code >= 0, 1.0, -1.0)


def stack_kernel(
    data_ref, place_ref, out_ref, wide, pairs, other, twin, goal_ref, mask_ref, held, acc
):
    inputs = data_ref.shape[0]
    half = inputs // 2
    lanes = data_ref.shape[1] - half
    blocks = lanes // 256
    width = lanes // SPECTRA
    steps = half // GROUP

    target, used, sign = decode(data_ref[:, lanes:])
    upper = target >= HALF_STACKS
    goal = jnp.where(upper, target - HALF_STACKS, target).astype(jnp.float32).T
    for g in range(steps):
        rolled = pltpu.roll(goal, (half - g * GROUP) % half, 1) if g else goal
        goal_ref[g * inputs : (g + 1) * inputs, :] = rolled
    left = jnp.where(used & ~upper, 1.0, 0.0)
    right = jnp.where(used & upper, 1.0, 0.0)
    for n, mask in enumerate((left, right, left * sign, right * sign)):
        mask_ref[n] = mask

    lane = lax.broadcasted_iota(jnp.int32, (half // 2, 128), 1)
    twin[...] = jnp.zeros(twin.shape, jnp.bfloat16)
    for b in range(blocks):
        other[b * 256 : (b + 1) * 256, :] = data_ref[:, b * 256 : (b + 1) * 256].T
        for m in range(2):
            tile = b * 2 + m
            wide[tile * inputs : (tile + 1) * inputs, :] = data_ref[
                :, tile * 128 : (tile + 1) * 128
            ].astype(jnp.float32)
            even = wide[pl.ds(tile * inputs + half, half // 2, stride=2), :]
            odd = wide[pl.ds(tile * inputs + half + 1, half // 2, stride=2), :]
            for part in range(2):
                if part == 0:
                    both = jnp.where(lane < 64, even, pltpu.roll(odd, 64, 1))
                else:
                    both = jnp.where(lane < 64, pltpu.roll(even, 64, 1), odd)
                at = (tile * 2 + part) * (half // 2)
                pairs[at : at + half // 2, :] = both
                source = slice(tile * 128 + part * 64, tile * 128 + part * 64 + 64)
                for side in range(2):
                    at = (b * 2 + part) * 256 + m * 128 + side * 64
                    twin[at : at + 64, side * half : (side + 1) * half] = other[source, half:]
    acc[...] = jnp.zeros(acc.shape, jnp.float32)

    def diagonal(rows):
        row = lax.broadcasted_iota(jnp.int32, (rows, 128), 0)
        lane = lax.broadcasted_iota(jnp.int32, (rows, 128), 1)
        channel = jnp.bitwise_and(lane, 15)
        if rows == 32:
            channel = channel + jnp.where(lane >= 64, 16, 0)
        return jnp.where(row == channel, 1.0, 0.0)

    diagonal_32, diagonal_16 = diagonal(32), diagonal(16)
    stack = lax.broadcasted_iota(jnp.int32, (inputs, HALF_STACKS), 1)
    stack = stack.astype(jnp.float32).astype(jnp.bfloat16)
    row = lax.broadcasted_iota(jnp.int32, (16, inputs), 0)
    first_row, second_row = row == 0, row == 1

    def spread(reals, imags, mask):
        parts = []
        for u in range(reals.shape[0]):
            real = mask * reals[u : u + 1]
            imag = mask * imags[u : u + 1]
            parts.append(jnp.concatenate([real, imag], axis=1))
            parts.append(jnp.concatenate([imag, -real], axis=1))
        return jnp.concatenate(parts, axis=0).astype(jnp.bfloat16)

    def multiply(g):
        start, start_pair = g * GROUP, g * GROUP // 2
        row = lax.broadcasted_iota(jnp.int32, (GROUP, half), 0) + start
        col = lax.broadcasted_iota(jnp.int32, (GROUP, half), 1)
        ahead = jnp.where(col > row, 1.0, 0.0)
        for b in range(blocks):
            rows = [wide[pl.ds((b * 2 + m) * inputs + start, GROUP), :] for m in range(2)]
            product = jnp.dot(
                spread(rows[0], rows[1], diagonal_32),
                other[b * 256 : (b + 1) * 256, :],
                preferred_element_type=jnp.float32,
            )
            lower = []
            for part in range(2):
                rows = [
                    pairs[
                        pl.ds(((b * 2 + m) * 2 + part) * (half // 2) + start_pair, GROUP // 2), :
                    ]
                    for m in range(2)
                ]
                at = (b * 2 + part) * 256
                lower.append(
                    jnp.dot(
                        spread(rows[0], rows[1], diagonal_16),
                        twin[at : at + 256, :],
                        preferred_element_type=jnp.float32,
                    )
                )
            for u in range(GROUP):
                side = slice((u % 2) * half, (u % 2 + 1) * half)
                use = jnp.broadcast_to(ahead[u : u + 1], (32, half)) > 0.5
                for p in range(2):
                    mine = product[u * 64 + p * 32 : u * 64 + p * 32 + 32]
                    at = (u // 2) * 32 + p * 16
                    low = jnp.concatenate([x[at : at + 16, side] for x in lower], axis=0)
                    chosen = jnp.where(use, mine[:, :half], low)
                    both = jnp.concatenate([chosen, mine[:, half:]], axis=1)
                    at = (p * blocks + b) * 32
                    held[at : at + 32, u * inputs : (u + 1) * inputs] = both.astype(jnp.bfloat16)

    def accumulate(g):
        start = g * GROUP
        goal = goal_ref[g * inputs : (g + 1) * inputs, :]
        masks = [mask_ref[n, pl.ds(start, GROUP), :].astype(jnp.bfloat16) for n in range(4)]
        members, values = [], []
        for u in range(GROUP):
            columns = slice(u * inputs, (u + 1) * inputs)
            left, right, left_sign, right_sign = [mask[u : u + 1] for mask in masks]
            real = held[: width // 2, columns]
            imag = held[width // 2 :, columns]
            tally = jnp.where(first_row, left, jnp.where(second_row, right, jnp.zeros_like(right)))
            values.append(
                jnp.concatenate(
                    [real * left, imag * left_sign, real * right, imag * right_sign, tally], axis=0
                )
            )
            mine = jnp.broadcast_to(goal[:, u : u + 1], stack.shape).astype(jnp.bfloat16)
            members.append(jnp.where(stack == mine, jnp.ones_like(stack), jnp.zeros_like(stack)))
        acc[...] += jnp.dot(
            jnp.concatenate(values, axis=1),
            jnp.concatenate(members, axis=0),
            preferred_element_type=jnp.float32,
        )

    multiply(0)
    for g in range(steps - 1):
        accumulate(g)
        multiply(g + 1)
    accumulate(steps - 1)

    means = []
    for n in range(2):
        counts = jnp.maximum(acc[2 * width + n : 2 * width + n + 1, :], 1.0)
        means.append((acc[n * width : (n + 1) * width, :] / counts).astype(jnp.bfloat16))
    moved = [
        lax.dot_general(
            place_ref[:, n * 256 : n * 256 + HALF_STACKS],
            means[n],
            (((1,), (1,)), ((), ())),
            preferred_element_type=jnp.float32,
        )
        for n in range(2)
    ]
    out_ref[...] = (moved[0] + moved[1]).astype(jnp.bfloat16)


def stack_means(data, place):
    inputs = data.shape[0]
    half = inputs // 2
    lanes = data.shape[1] - half
    width = lanes // SPECTRA
    return pl.pallas_call(
        stack_kernel,
        out_shape=jax.ShapeDtypeStruct((place.shape[0], width), jnp.bfloat16),
        scratch_shapes=[
            pltpu.VMEM((lanes // 128 * inputs, 128), jnp.float32),
            pltpu.VMEM((lanes // 128 * half, 128), jnp.float32),
            pltpu.VMEM((lanes, inputs), jnp.bfloat16),
            pltpu.VMEM((2 * lanes, inputs), jnp.bfloat16),
            pltpu.VMEM((half // GROUP * inputs, half), jnp.float32),
            pltpu.VMEM((4, half, inputs), jnp.float32),
            pltpu.VMEM((width, GROUP * inputs), jnp.bfloat16),
            pltpu.VMEM((2 * width + 16, HALF_STACKS), jnp.float32),
        ],
        compiler_params=pltpu.CompilerParams(vmem_limit_bytes=48 * MB),
        name="stack_means",
    )(data, place)


def lay_out_kernel(feeds, padded, capacity, landed_ref, out_ref):
    lane = lax.broadcasted_iota(jnp.int32, (padded, 128), 1)
    for pair in range(feeds // 2):
        left = landed_ref[2 * pair * padded : (2 * pair + 1) * padded, :].astype(jnp.float32)
        right = landed_ref[(2 * pair + 1) * padded : (2 * pair + 2) * padded, :].astype(
            jnp.float32
        )
        real = jnp.where(lane < 64, left, pltpu.roll(right, 64, 1))
        imag = jnp.where(lane < 64, pltpu.roll(left, 64, 1), right)
        for part, value in enumerate((real, imag)):
            out_ref[pl.ds(pair * 2 + part, capacity, stride=feeds), :] = value[:capacity]


def lay_out(landed, feeds, padded, capacity):
    return pl.pallas_call(
        functools.partial(lay_out_kernel, feeds, padded, capacity),
        out_shape=jax.ShapeDtypeStruct((capacity * feeds, 128), jnp.float32),
        compiler_params=pltpu.CompilerParams(vmem_limit_bytes=32 * MB),
        name="lay_out",
    )(landed)


def per_device(raw_samples, stack_code, stack_owner):
    feeds, chans = lax.axis_size("feed"), lax.axis_size("chan")
    devices = feeds * chans
    inputs = raw_samples.shape[0]
    half = stack_code.shape[1] // 2
    everyone = ("feed", "chan")
    share = CHANS // devices
    capacity = 2 * STACKS // feeds
    padded = -(-capacity // 16) * 16
    direct = share == FA and inputs == 8

    owner = jnp.pad(
        stack_owner.astype(jnp.float32), (0, STACK_ROWS - STACKS), constant_values=-1.0
    ).reshape(1, STACK_ROWS)
    place = place_stacks(owner, padded, feeds)

    if direct:
        order = [c * feeds + f for f in range(feeds) for c in range(chans)]
        local = channelize(raw_samples, stack_code, order, True)
        local = local.reshape(devices, inputs, -1)
    else:
        samples = jnp.pad(raw_samples, ((0, -inputs % 8), (0, 0)))
        codes = lax.dynamic_slice_in_dim(stack_code, lax.axis_index("chan") * inputs, inputs)
        codes = jnp.pad(codes, ((0, -inputs % 8), (0, 0)))
        local = channelize(samples, codes, list(range(QS)), False)
        local = local.reshape(QS, samples.shape[0], -1)[:, :inputs]
        codes = jnp.broadcast_to(local[:1, :, 512:], (devices, inputs, half))
        local = local[:, :, :512].reshape(QS, inputs, 2, 2, 2, SPECTRA, 16)
        local = local.transpose(0, 2, 4, 6, 1, 3, 5)
        local = local.reshape(chans, feeds, share // 16, 16, inputs, 2, SPECTRA)
        local = local.transpose(1, 0, 4, 5, 2, 6, 3).reshape(devices, inputs, 8 * share)
        local = jnp.concatenate([local, codes], axis=2)
    moved = lax.all_to_all(local, everyone, split_axis=0, concat_axis=0, tiled=True)
    if not direct:
        codes = moved[:, :, 8 * share :]
        moved = moved[:, :, : 8 * share].reshape(devices, inputs, 2, 4 * share)
        moved = jnp.pad(moved, ((0, 0), (0, 0), (0, 0), (0, 128 - 4 * share)))
        moved = jnp.concatenate([moved.reshape(devices, inputs, 256), codes], axis=2)
    moved = moved.reshape(devices * inputs, -1)

    means = stack_means(moved, place)
    landed = lax.all_to_all(
        means.reshape(feeds, padded, -1), "feed", split_axis=0, concat_axis=0, tiled=True
    )
    if direct:
        landed = lay_out(landed.reshape(feeds * padded, -1), feeds, padded, capacity)
        landed = landed.reshape(capacity, feeds // 2, 2, 128).transpose(0, 2, 1, 3)
        return landed.reshape(capacity, 2, feeds * share)
    landed = landed[:, :capacity].reshape(feeds, capacity, 2, -1)[..., :share]
    return landed.transpose(1, 2, 0, 3).reshape(capacity, 2, feeds * share).astype(jnp.float32)


def solution(mesh):
    placed = (P(("feed", "chan"), None), P("feed", None), P())
    return jax.shard_map(
        per_device, mesh=mesh, in_specs=placed, out_specs=P("feed", None, "chan"), check_vma=False
    )
```

```python
import functools
import math

import jax
import jax.numpy as jnp
import numpy as np
from jax import lax
from jax.experimental import pallas as pl
from jax.experimental.pallas import tpu as pltpu
from jax.sharding import PartitionSpec as P

SPECTRA = 4
TAPS = 8
FA = 64
FB = 128
FRAME = 8192
CHANS = 2048
STACKS = 382
QS = CHANS // FA
STACK_ROWS = 384
HALF_STACKS = 192
GROUP = 16
PIECES = 2
CODE_BASE = 384
MB = 1024 * 1024


def window_table():
    length = TAPS * FRAME
    sample = np.arange(length, dtype=np.float64)
    centred = (sample - length / 2 + 0.5) / FRAME
    hanning = 0.5 - 0.5 * np.cos(2.0 * np.pi * (sample + 0.5) / length)
    weights = np.sinc(centred) * hanning
    weights = weights * np.sqrt(FRAME / np.sum(weights * weights))
    return weights.reshape(TAPS, FRAME).astype(np.float32)


def angle_of(left_count, right_count, modulus):
    product = np.arange(left_count)[:, None] * np.arange(right_count)[None, :] % modulus
    return 2.0 * np.pi * product / modulus


def first_table():
    angles = angle_of(FA, FA, FA)
    return np.concatenate([np.cos(angles), -np.sin(angles)], axis=0)


def twiddles():
    angles = angle_of(FA, FB, FRAME)
    return np.cos(angles).astype(np.float32), np.sin(angles).astype(np.float32)


def second_table(order):
    angles = angle_of(FB, QS, FB).T[np.asarray(order)]
    cosine, sine = np.cos(angles), np.sin(angles)
    real_rows = np.concatenate([cosine, sine], axis=1)
    imag_rows = np.concatenate([-sine, cosine], axis=1)
    return np.concatenate([real_rows, imag_rows], axis=0)


def channelize_kernel(
    direct, x_hbm, code_hbm, window_hbm, first_hbm, cos_hbm, sin_hbm, second_hbm, out_ref,
    x_ref, code_ref, window_ref, first_ref, cos_ref, sin_ref, second_ref, frames, mixed, turned,
    x_sems, sems,
):
    inputs = x_ref.shape[0]
    piece = FRAME // PIECES
    pieces = []
    for k in range(PIECES):
        window_copy = pltpu.make_async_copy(
            window_hbm.at[:, k * piece : (k + 1) * piece],
            window_ref.at[:, k * piece : (k + 1) * piece],
            x_sems.at[k, 0],
        )
        window_copy.start()
        copies = [window_copy]
        for r in range(SPECTRA + TAPS - 1):
            at = slice(r * FRAME + k * piece, r * FRAME + (k + 1) * piece)
            copy = pltpu.make_async_copy(x_hbm.at[:, at], x_ref.at[:, at], x_sems.at[k, 1 + r])
            copy.start()
            copies.append(copy)
        pieces.append(copies)
    others = []
    for n, (source, target) in enumerate(
        [
            (code_hbm, code_ref),
            (first_hbm, first_ref),
            (cos_hbm, cos_ref),
            (sin_hbm, sin_ref),
            (second_hbm, second_ref),
        ]
    ):
        copy = pltpu.make_async_copy(source, target, sems.at[n])
        copy.start()
        others.append(copy)

    for a in range(FA):
        if a % (FA // PIECES) == 0:
            for copy in pieces[a // (FA // PIECES)]:
                copy.wait()
        sums = [None] * SPECTRA
        for r in range(SPECTRA + TAPS - 1):
            x = x_ref[:, r * FRAME + a * FB : r * FRAME + (a + 1) * FB].astype(jnp.float32)
            for t in range(SPECTRA):
                if 0 <= r - t < TAPS:
                    term = window_ref[r - t : r - t + 1, a * FB : (a + 1) * FB] * x
                    sums[t] = term if sums[t] is None else sums[t] + term
        for t in range(SPECTRA):
            frames[(t * FA + a) * inputs : (t * FA + a + 1) * inputs, :] = sums[t]
    for copy in others:
        copy.wait()

    count = code_ref.shape[1]
    half = count // 2
    place = lax.axis_index("feed") * lax.axis_size("chan") + lax.axis_index("chan")
    if direct:
        start = pl.multiple_of(lax.axis_index("chan") * inputs, 8)
        codes = code_ref[pl.ds(start, inputs), :]
        first_input = place * inputs
    else:
        codes = code_ref[...]
        first_input = place * (count // (lax.axis_size("feed") * lax.axis_size("chan")))
    row = lax.broadcasted_iota(jnp.int32, (inputs, half), 0) + first_input
    col = lax.broadcasted_iota(jnp.int32, (inputs, half), 1)
    apart = jnp.bitwise_and(col - row, count - 1)
    code = jnp.where((apart >= 1) & (apart <= half), codes[:, :half], codes[:, half:])
    shifted = code + CODE_BASE
    code = jnp.left_shift(128 + jnp.bitwise_and(shifted, 127), jnp.right_shift(shifted, 7))
    code = code.astype(jnp.float32)
    out_ref[:, 512:] = jnp.concatenate([code] * QS, axis=0).astype(jnp.bfloat16)

    for t in range(SPECTRA):
        wide = [frames[pl.ds(t * FA * inputs + i, FA, stride=inputs), :] for i in range(inputs)]
        wide = jnp.concatenate([part.astype(jnp.bfloat16) for part in wide], axis=1)
        section = jnp.dot(first_ref[...], wide, preferred_element_type=jnp.float32)
        for i in range(inputs):
            real = section[:FA, i * FB : (i + 1) * FB]
            imag = section[FA:, i * FB : (i + 1) * FB]
            cosine, sine = cos_ref[...], sin_ref[...]
            twisted = jnp.concatenate(
                [real * cosine + imag * sine, imag * cosine - real * sine], axis=1
            ).astype(jnp.bfloat16)
            for part in range(4):
                start = (i * 4 + part) * 64 + t * 16
                mixed[start : start + 16, :] = twisted[part * 16 : (part + 1) * 16]
    for i in range(inputs):
        spectra = lax.dot_general(
            second_ref[...],
            mixed[i * 256 : (i + 1) * 256, :],
            (((1,), (1,)), ((), ())),
            preferred_element_type=jnp.float32,
        ) * (1.0 / math.sqrt(FRAME))
        for m in range(2):
            for g in range(QS // 8):
                for h in range(2):
                    tile = spectra[m * QS + g * 8 : m * QS + g * 8 + 8, h * 128 : (h + 1) * 128]
                    start = ((h * 2 + m) * QS + g * 8) * inputs + i
                    turned[pl.ds(start, 8, stride=inputs), :] = tile
    for part in range(4):
        rows = turned[part * QS * inputs : (part + 1) * QS * inputs, :]
        out_ref[:, part * 128 : (part + 1) * 128] = rows.astype(jnp.bfloat16)


def channelize(samples, codes, order, direct):
    inputs = samples.shape[0]
    cosine, sine = twiddles()
    operands = (
        samples,
        codes,
        jnp.asarray(window_table()),
        jnp.asarray(first_table(), jnp.bfloat16),
        jnp.asarray(cosine),
        jnp.asarray(sine),
        jnp.asarray(second_table(order), jnp.bfloat16),
    )
    return pl.pallas_call(
        functools.partial(channelize_kernel, direct),
        out_shape=jax.ShapeDtypeStruct((QS * inputs, 512 + codes.shape[1] // 2), jnp.bfloat16),
        in_specs=[pl.BlockSpec(memory_space=pl.ANY)] * len(operands),
        scratch_shapes=[pltpu.VMEM(value.shape, value.dtype) for value in operands]
        + [
            pltpu.VMEM((SPECTRA * inputs * FA, FB), jnp.float32),
            pltpu.VMEM((SPECTRA * inputs * FA, 2 * FB), jnp.bfloat16),
            pltpu.VMEM((4 * QS * inputs, 128), jnp.float32),
            pltpu.SemaphoreType.DMA((PIECES, SPECTRA + TAPS)),
            pltpu.SemaphoreType.DMA((5,)),
        ],
        compiler_params=pltpu.CompilerParams(vmem_limit_bytes=56 * MB),
        name="channelize",
    )(*operands)


def place_kernel(padded, owner_ref, place_ref):
    owner = owner_ref[...]
    across = jnp.broadcast_to(owner, (STACK_ROWS, STACK_ROWS))
    down = across.T
    before = lax.broadcasted_iota(jnp.int32, (STACK_ROWS, STACK_ROWS), 0)
    after = lax.broadcasted_iota(jnp.int32, (STACK_ROWS, STACK_ROWS), 1)
    earlier = jnp.where((across == down) & (before < after), 1.0, 0.0)
    rank = jnp.sum(earlier, axis=0, keepdims=True)
    slot = jnp.where(owner >= 0, owner * padded, -STACK_ROWS) + rank
    slot_id = lax.broadcasted_iota(jnp.int32, (place_ref.shape[0], STACK_ROWS), 0)
    place = jnp.where(slot_id.astype(jnp.float32) == slot, 1.0, 0.0)
    place_ref[...] = jnp.zeros(place_ref.shape, jnp.bfloat16)
    for n in range(2):
        half = place[:, n * HALF_STACKS : (n + 1) * HALF_STACKS].astype(jnp.bfloat16)
        place_ref[:, n * 256 : n * 256 + HALF_STACKS] = half


def place_stacks(owner, padded, feeds):
    return pl.pallas_call(
        functools.partial(place_kernel, padded),
        out_shape=jax.ShapeDtypeStruct((feeds * padded, 512), jnp.bfloat16),
        compiler_params=pltpu.CompilerParams(vmem_limit_bytes=16 * MB),
        name="place_stacks",
    )(owner)


def decode(codes):
    inputs = codes.shape[0]
    half = inputs // 2
    value = codes.astype(jnp.float32).astype(jnp.int32)
    power = jnp.zeros(value.shape, jnp.int32)
    for e in range(1, 6):
        power = power + jnp.where(value >= 128 << e, 1, 0)
    code = power * 128 + jnp.right_shift(value, power) - 128 - CODE_BASE
    row = lax.broadcasted_iota(jnp.int32, (half, half), 0)
    col = lax.broadcasted_iota(jnp.int32, (half, half), 1)
    ahead = col > row
    low = code[:half]
    high = -1 - code[half:].astype(jnp.float32).T.astype(jnp.int32)
    code = jnp.concatenate([jnp.where(ahead, low, high), jnp.where(ahead, high, low)], axis=1)
    target = jnp.where(code >= 0, code, -1 - code)
    row = lax.broadcasted_iota(jnp.int32, (half, inputs), 0)
    col = lax.broadcasted_iota(jnp.int32, (half, inputs), 1)
    return target, col != row, jnp.where(code >= 0, 1.0, -1.0)


def stack_kernel(
    data_ref, place_ref, out_ref, wide, pairs, other, twin, goal_ref, mask_ref, held, acc
):
    inputs = data_ref.shape[0]
    half = inputs // 2
    lanes = data_ref.shape[1] - half
    blocks = lanes // 256
    width = lanes // SPECTRA
    steps = half // GROUP

    target, used, sign = decode(data_ref[:, lanes:])
    upper = target >= HALF_STACKS
    goal = jnp.where(upper, target - HALF_STACKS, target).astype(jnp.float32).T
    for g in range(steps):
        rolled = pltpu.roll(goal, (half - g * GROUP) % half, 1) if g else goal
        goal_ref[g * inputs : (g + 1) * inputs, :] = rolled
    left = jnp.where(used & ~upper, 1.0, 0.0)
    right = jnp.where(used & upper, 1.0, 0.0)
    for n, mask in enumerate((left, right, left * sign, right * sign)):
        mask_ref[n] = mask

    lane = lax.broadcasted_iota(jnp.int32, (half // 2, 128), 1)
    twin[...] = jnp.zeros(twin.shape, jnp.bfloat16)
    for b in range(blocks):
        other[b * 256 : (b + 1) * 256, :] = data_ref[:, b * 256 : (b + 1) * 256].T
        for m in range(2):
            tile = b * 2 + m
            wide[tile * inputs : (tile + 1) * inputs, :] = data_ref[
                :, tile * 128 : (tile + 1) * 128
            ].astype(jnp.float32)
            even = wide[pl.ds(tile * inputs + half, half // 2, stride=2), :]
            odd = wide[pl.ds(tile * inputs + half + 1, half // 2, stride=2), :]
            for part in range(2):
                if part == 0:
                    both = jnp.where(lane < 64, even, pltpu.roll(odd, 64, 1))
                else:
                    both = jnp.where(lane < 64, pltpu.roll(even, 64, 1), odd)
                at = (tile * 2 + part) * (half // 2)
                pairs[at : at + half // 2, :] = both
                source = slice(tile * 128 + part * 64, tile * 128 + part * 64 + 64)
                for side in range(2):
                    at = (b * 2 + part) * 256 + m * 128 + side * 64
                    twin[at : at + 64, side * half : (side + 1) * half] = other[source, half:]
    acc[...] = jnp.zeros(acc.shape, jnp.float32)

    def diagonal(rows):
        row = lax.broadcasted_iota(jnp.int32, (rows, 128), 0)
        lane = lax.broadcasted_iota(jnp.int32, (rows, 128), 1)
        channel = jnp.bitwise_and(lane, 15)
        if rows == 32:
            channel = channel + jnp.where(lane >= 64, 16, 0)
        return jnp.where(row == channel, 1.0, 0.0)

    diagonal_32, diagonal_16 = diagonal(32), diagonal(16)
    stack = lax.broadcasted_iota(jnp.int32, (inputs, HALF_STACKS), 1)
    stack = stack.astype(jnp.float32).astype(jnp.bfloat16)
    row = lax.broadcasted_iota(jnp.int32, (16, inputs), 0)
    first_row, second_row = row == 0, row == 1

    def spread(reals, imags, mask):
        parts = []
        for u in range(reals.shape[0]):
            real = mask * reals[u : u + 1]
            imag = mask * imags[u : u + 1]
            parts.append(jnp.concatenate([real, imag], axis=1))
            parts.append(jnp.concatenate([imag, -real], axis=1))
        return jnp.concatenate(parts, axis=0).astype(jnp.bfloat16)

    def multiply(g):
        start, start_pair = g * GROUP, g * GROUP // 2
        row = lax.broadcasted_iota(jnp.int32, (GROUP, half), 0) + start
        col = lax.broadcasted_iota(jnp.int32, (GROUP, half), 1)
        ahead = jnp.where(col > row, 1.0, 0.0)
        for b in range(blocks):
            rows = [wide[pl.ds((b * 2 + m) * inputs + start, GROUP), :] for m in range(2)]
            product = jnp.dot(
                spread(rows[0], rows[1], diagonal_32),
                other[b * 256 : (b + 1) * 256, :],
                preferred_element_type=jnp.float32,
            )
            lower = []
            for part in range(2):
                rows = [
                    pairs[
                        pl.ds(((b * 2 + m) * 2 + part) * (half // 2) + start_pair, GROUP // 2), :
                    ]
                    for m in range(2)
                ]
                at = (b * 2 + part) * 256
                lower.append(
                    jnp.dot(
                        spread(rows[0], rows[1], diagonal_16),
                        twin[at : at + 256, :],
                        preferred_element_type=jnp.float32,
                    )
                )
            for u in range(GROUP):
                side = slice((u % 2) * half, (u % 2 + 1) * half)
                use = jnp.broadcast_to(ahead[u : u + 1], (32, half)) > 0.5
                for p in range(2):
                    mine = product[u * 64 + p * 32 : u * 64 + p * 32 + 32]
                    at = (u // 2) * 32 + p * 16
                    low = jnp.concatenate([x[at : at + 16, side] for x in lower], axis=0)
                    chosen = jnp.where(use, mine[:, :half], low)
                    both = jnp.concatenate([chosen, mine[:, half:]], axis=1)
                    at = (p * blocks + b) * 32
                    held[g % 2, at : at + 32, u * inputs : (u + 1) * inputs] = both.astype(jnp.bfloat16)

    def accumulate(g):
        start = g * GROUP
        goal = goal_ref[g * inputs : (g + 1) * inputs, :]
        masks = [mask_ref[n, pl.ds(start, GROUP), :].astype(jnp.bfloat16) for n in range(4)]
        members, values = [], []
        for u in range(GROUP):
            columns = slice(u * inputs, (u + 1) * inputs)
            left, right, left_sign, right_sign = [mask[u : u + 1] for mask in masks]
            real = held[g % 2, : width // 2, columns]
            imag = held[g % 2, width // 2 :, columns]
            tally = jnp.where(first_row, left, jnp.where(second_row, right, jnp.zeros_like(right)))
            values.append(
                jnp.concatenate(
                    [real * left, imag * left_sign, real * right, imag * right_sign, tally], axis=0
                )
            )
            mine = jnp.broadcast_to(goal[:, u : u + 1], stack.shape).astype(jnp.bfloat16)
            members.append(jnp.where(stack == mine, jnp.ones_like(stack), jnp.zeros_like(stack)))
        acc[...] += jnp.dot(
            jnp.concatenate(values, axis=1),
            jnp.concatenate(members, axis=0),
            preferred_element_type=jnp.float32,
        )

    multiply(0)
    for g in range(steps - 1):
        multiply(g + 1)
        accumulate(g)
    accumulate(steps - 1)

    means = []
    for n in range(2):
        counts = jnp.maximum(acc[2 * width + n : 2 * width + n + 1, :], 1.0)
        means.append((acc[n * width : (n + 1) * width, :] / counts).astype(jnp.bfloat16))
    moved = [
        lax.dot_general(
            place_ref[:, n * 256 : n * 256 + HALF_STACKS],
            means[n],
            (((1,), (1,)), ((), ())),
            preferred_element_type=jnp.float32,
        )
        for n in range(2)
    ]
    out_ref[...] = (moved[0] + moved[1]).astype(jnp.bfloat16)


def stack_means(data, place):
    inputs = data.shape[0]
    half = inputs // 2
    lanes = data.shape[1] - half
    width = lanes // SPECTRA
    return pl.pallas_call(
        stack_kernel,
        out_shape=jax.ShapeDtypeStruct((place.shape[0], width), jnp.bfloat16),
        scratch_shapes=[
            pltpu.VMEM((lanes // 128 * inputs, 128), jnp.float32),
            pltpu.VMEM((lanes // 128 * half, 128), jnp.float32),
            pltpu.VMEM((lanes, inputs), jnp.bfloat16),
            pltpu.VMEM((2 * lanes, inputs), jnp.bfloat16),
            pltpu.VMEM((half // GROUP * inputs, half), jnp.float32),
            pltpu.VMEM((4, half, inputs), jnp.float32),
            pltpu.VMEM((2, width, GROUP * inputs), jnp.bfloat16),
            pltpu.VMEM((2 * width + 16, HALF_STACKS), jnp.float32),
        ],
        compiler_params=pltpu.CompilerParams(vmem_limit_bytes=48 * MB),
        name="stack_means",
    )(data, place)


def lay_out_kernel(feeds, padded, capacity, landed_ref, out_ref):
    lane = lax.broadcasted_iota(jnp.int32, (padded, 128), 1)
    for pair in range(feeds // 2):
        left = landed_ref[2 * pair * padded : (2 * pair + 1) * padded, :].astype(jnp.float32)
        right = landed_ref[(2 * pair + 1) * padded : (2 * pair + 2) * padded, :].astype(
            jnp.float32
        )
        real = jnp.where(lane < 64, left, pltpu.roll(right, 64, 1))
        imag = jnp.where(lane < 64, pltpu.roll(left, 64, 1), right)
        for part, value in enumerate((real, imag)):
            out_ref[pl.ds(pair * 2 + part, capacity, stride=feeds), :] = value[:capacity]


def lay_out(landed, feeds, padded, capacity):
    return pl.pallas_call(
        functools.partial(lay_out_kernel, feeds, padded, capacity),
        out_shape=jax.ShapeDtypeStruct((capacity * feeds, 128), jnp.float32),
        compiler_params=pltpu.CompilerParams(vmem_limit_bytes=32 * MB),
        name="lay_out",
    )(landed)


def per_device(raw_samples, stack_code, stack_owner):
    feeds, chans = lax.axis_size("feed"), lax.axis_size("chan")
    devices = feeds * chans
    inputs = raw_samples.shape[0]
    half = stack_code.shape[1] // 2
    everyone = ("feed", "chan")
    share = CHANS // devices
    capacity = 2 * STACKS // feeds
    padded = -(-capacity // 16) * 16
    direct = share == FA and inputs == 8

    owner = jnp.pad(
        stack_owner.astype(jnp.float32), (0, STACK_ROWS - STACKS), constant_values=-1.0
    ).reshape(1, STACK_ROWS)
    place = place_stacks(owner, padded, feeds)

    if direct:
        order = [c * feeds + f for f in range(feeds) for c in range(chans)]
        local = channelize(raw_samples, stack_code, order, True)
        local = local.reshape(devices, inputs, -1)
    else:
        samples = jnp.pad(raw_samples, ((0, -inputs % 8), (0, 0)))
        codes = lax.dynamic_slice_in_dim(stack_code, lax.axis_index("chan") * inputs, inputs)
        codes = jnp.pad(codes, ((0, -inputs % 8), (0, 0)))
        local = channelize(samples, codes, list(range(QS)), False)
        local = local.reshape(QS, samples.shape[0], -1)[:, :inputs]
        codes = jnp.broadcast_to(local[:1, :, 512:], (devices, inputs, half))
        local = local[:, :, :512].reshape(QS, inputs, 2, 2, 2, SPECTRA, 16)
        local = local.transpose(0, 2, 4, 6, 1, 3, 5)
        local = local.reshape(chans, feeds, share // 16, 16, inputs, 2, SPECTRA)
        local = local.transpose(1, 0, 4, 5, 2, 6, 3).reshape(devices, inputs, 8 * share)
        local = jnp.concatenate([local, codes], axis=2)
    moved = lax.all_to_all(local, everyone, split_axis=0, concat_axis=0, tiled=True)
    if not direct:
        codes = moved[:, :, 8 * share :]
        moved = moved[:, :, : 8 * share].reshape(devices, inputs, 2, 4 * share)
        moved = jnp.pad(moved, ((0, 0), (0, 0), (0, 0), (0, 128 - 4 * share)))
        moved = jnp.concatenate([moved.reshape(devices, inputs, 256), codes], axis=2)
    moved = moved.reshape(devices * inputs, -1)

    means = stack_means(moved, place)
    landed = lax.all_to_all(
        means.reshape(feeds, padded, -1), "feed", split_axis=0, concat_axis=0, tiled=True
    )
    if direct:
        landed = lay_out(landed.reshape(feeds * padded, -1), feeds, padded, capacity)
        landed = landed.reshape(capacity, feeds // 2, 2, 128).transpose(0, 2, 1, 3)
        return landed.reshape(capacity, 2, feeds * share)
    landed = landed[:, :capacity].reshape(feeds, capacity, 2, -1)[..., :share]
    return landed.transpose(1, 2, 0, 3).reshape(capacity, 2, feeds * share).astype(jnp.float32)


def solution(mesh):
    placed = (P(("feed", "chan"), None), P("feed", None), P())
    return jax.shard_map(
        per_device, mesh=mesh, in_specs=placed, out_specs=P("feed", None, "chan"), check_vma=False
    )
```
